256 devices in a mesh: face: 4 (over z_hi), row: 8 (over y, core), col: 8 (over z_lo, x).
Axes of the slice: x: 4, y: 4, z: 8 (z_hi: 4, z_lo: 2; z = z_hi * 2 + z_lo), core: 2. Of those that a mesh axis runs over, the one named last changes fastest.
Arguments:
- field: bfloat16 [12, 512, 512, 128], P('face', 'row', 'col'), may hold values from -6 to 6
- conv1_w: bfloat16 [3, 3, 128, 128], replicated, may hold values from -0.1875 to 0.1875
- conv1_b: float32 [128], replicated, may hold values from -3 to 3
- conv2_w: bfloat16 [3, 3, 128, 128], replicated, may hold values from -0.1875 to 0.1875
- conv2_b: float32 [128], replicated, may hold values from -3 to 3
- down_w: bfloat16 [2, 2, 128, 256], replicated, may hold values from -0.25 to 0.25
- down_b: float32 [256], replicated, may hold values from -3 to 3
- neighbour_face: int32 [12, 8], replicated, may hold values from 0 to 12, as said below
- orientation: int32 [12, 8], replicated, may hold values from 0 to 7, as said below
Outputs:
- skip: bfloat16 [12, 512, 512, 128], P('face', 'row', 'col')
- coarse: bfloat16 [12, 256, 256, 256], P('face', 'row', 'col')
The draws below stay inside these ranges and needn't reach their ends.
Inputs may be any that keep to these rules, and one draw needn't show every extreme that they name: `neighbour_face`: entries 0 to 3 of a row name the face across the top, right, bottom and left edge; entries 4 to 7 name the face diagonally across the top-left, top-right, bottom-right and bottom-left corner point, or 12 where only three faces meet there. Edge neighbours are mutual: if face f names face n across edge e, face n names f across the edge that orientation gives. `orientation`: entries 0 to 3 are 2 * e + r, where e is the neighbour's edge (0 top, 1 right, 2 bottom, 3 left) that meets this edge and r is 1 where positions along the two edges run opposite ways; entries 4 to 7 are the neighbour's corner (0 top-left, 1 top-right, 2 bottom-right, 3 bottom-left) that touches this corner, 0 where there is no such neighbour.
All inputs are finite; a program needn't handle non-finite values.
Results may differ from the reference program's by a relative error of at most 0.005.
Values may be sent and summed in bfloat16 or wider, within the bound.
A program may use at most 128 MiB of HBM per device.

```python
import jax
import jax.numpy as jnp
import numpy as np
from jax import lax

FACES = 12
CH = 128
CO = 256
SIDE = 512


def dihedral_tables():
    normals = [(-1, 0), (0, 1), (1, 0), (0, -1)]
    alongs = [(0, 1), (1, 0), (0, 1), (1, 0)]
    points = [(-1, -1), (-1, 1), (1, 1), (1, -1)]
    edge_map = np.zeros((8, 4), np.int32)
    edge_rev = np.zeros((8, 4), np.int32)
    corner_map = np.zeros((8, 4), np.int32)
    for turning in range(8):

        def moved(vector):
            row_step, col_step = vector
            if turning >= 4:
                row_step, col_step = (col_step, row_step)
            for quarter in range(turning % 4):
                row_step, col_step = (col_step, -row_step)
            return (row_step, col_step)
        for which in range(4):
            target = normals.index(moved(normals[which]))
            edge_map[turning, which] = target
            edge_rev[turning, which] = int(moved(alongs[which]) != alongs[target])
            corner_map[turning, which] = points.index(moved(points[which]))
    edge_inverse = np.argsort(edge_map, axis=1).astype(np.int32)
    corner_inverse = np.argsort(corner_map, axis=1).astype(np.int32)
    return (edge_map, edge_rev, corner_map, edge_inverse, corner_inverse)


def base_links():
    edge_face = np.zeros((12, 4), np.int32)
    edge_side = np.zeros((12, 4), np.int32)
    corner_face = np.full((12, 4), 12, np.int32)
    corner_point = np.zeros((12, 4), np.int32)
    for which in range(4):
        following = (which + 1) % 4
        preceding = (which + 3) % 4
        opposite = (which + 2) % 4
        edge_face[which] = [following, 4 + following, 4 + which, preceding]
        edge_side[which] = [3, 3, 0, 0]
        edge_face[4 + which] = [which, 8 + which, 8 + preceding, preceding]
        edge_side[4 + which] = [2, 3, 0, 1]
        edge_face[8 + which] = [4 + following, 8 + following, 8 + preceding, 4 + which]
        edge_side[8 + which] = [2, 2, 1, 1]
        corner_face[which, 0] = opposite
        corner_point[which, 0] = 0
        corner_face[which, 2] = 8 + which
        corner_point[which, 2] = 0
        corner_face[4 + which, 1] = 4 + following
        corner_point[4 + which, 1] = 3
        corner_face[4 + which, 3] = 4 + preceding
        corner_point[4 + which, 3] = 1
        corner_face[8 + which, 0] = which
        corner_point[8 + which, 0] = 2
        corner_face[8 + which, 2] = 8 + opposite
        corner_point[8 + which, 2] = 2
    return (edge_face, edge_side, corner_face, corner_point)


def linked(key):
    edge_map, edge_rev, corner_map, edge_inverse, corner_inverse = [jnp.asarray(table) for table in dihedral_tables()]
    edge_face, edge_side, corner_face, corner_point = [jnp.asarray(table) for table in base_links()]
    placing = jax.random.permutation(jax.random.fold_in(key, 11), 12).astype(jnp.int32)
    turning = jax.random.randint(jax.random.fold_in(key, 12), (12,), 0, 8).astype(jnp.int32)
    slot_of = jnp.zeros((12,), jnp.int32).at[placing].set(jnp.arange(12, dtype=jnp.int32))
    sides = jnp.arange(4, dtype=jnp.int32)[None, :]
    own_turn = turning[:, None]
    base_face = placing[:, None]
    base_side = edge_inverse[own_turn, sides]
    far_base = edge_face[base_face, base_side]
    far_base_side = edge_side[base_face, base_side]
    far_slot = slot_of[far_base]
    far_turn = turning[far_slot]
    far_side = edge_map[far_turn, far_base_side]
    flipped = (edge_rev[own_turn, base_side] + edge_rev[far_turn, far_base_side]) % 2
    base_point = corner_inverse[own_turn, sides]
    corner_base = corner_face[base_face, base_point]
    present = corner_base < 12
    corner_slot = jnp.where(present, slot_of[jnp.minimum(corner_base, 11)], 12)
    corner_turn = turning[jnp.minimum(corner_slot, 11)]
    corner_code = jnp.where(present, corner_map[corner_turn, corner_point[base_face, base_point]], 0)
    faces = jnp.concatenate([far_slot, corner_slot], axis=1).astype(jnp.int32)
    codes = jnp.concatenate([2 * far_side + flipped, corner_code], axis=1).astype(jnp.int32)
    return (faces, codes)


def draw_neighbour_face(key, part):
    return linked(key)[0]


def draw_orientation(key, part):
    return linked(key)[1]


def levels(key, shape, shards, smallest, high):
    level, own = 1.0, jax.random.fold_in(key, 6)
    for dim, blocks in shards:
        draws = jnp.exp(jax.random.uniform(jax.random.fold_in(own, dim), (blocks,), jnp.float32, smallest / len(shards), high / len(shards)))
        level = level * jnp.repeat(draws, shape[dim] // blocks).reshape([-1 if axis == dim else 1 for axis in range(len(shape))])
    return level


def noise(rng, extent, spread, reach, pieces=(), kind=jnp.bfloat16):
    drawn = jax.random.normal(rng, extent, jnp.float32) * spread
    if len(pieces) > 0:
        drawn = levels(rng, extent, pieces, -0.22, 0.18) * drawn
    return jnp.clip(drawn, min=-reach, max=reach).astype(kind)


def setup_inputs(seed: int = 0) -> dict:
    arg_keys = jax.random.split(jax.random.key(seed), 10)
    return {
        "field": noise(arg_keys[0], (FACES, SIDE, SIDE, CH), 1.0, 6.0, ((0, 4), (1, 8), (2, 8))),
        "conv1_w": noise(arg_keys[1], (3, 3, CH, CH), (9 * CH) ** -0.5, 0.1875),
        "conv1_b": noise(arg_keys[2], (CH,), 0.5, 3.0, (), jnp.float32),
        "conv2_w": noise(arg_keys[3], (3, 3, CH, CH), (9 * CH) ** -0.5, 0.1875),
        "conv2_b": noise(arg_keys[4], (CH,), 0.5, 3.0, (), jnp.float32),
        "down_w": noise(arg_keys[5], (2, 2, CH, CO), (4 * CH) ** -0.5, 0.25),
        "down_b": noise(arg_keys[6], (CO,), 0.5, 3.0, (), jnp.float32),
        "neighbour_face": draw_neighbour_face(jax.random.fold_in(arg_keys[9], 71), 0),
        "orientation": draw_orientation(jax.random.fold_in(arg_keys[9], 71), 0),
    }


layout = ("NHWC", "HWIO", "NHWC")


def face_edges(values):
    return jnp.stack([values[:, 0], values[:, :, -1], values[:, -1], values[:, :, 0]], axis=1)


def seam_parts(edges, neighbours, codes):
    seam_faces = neighbours[:, :4]
    seam_codes = codes[:, :4]
    seams = edges[seam_faces, seam_codes // 2]
    seams = jnp.where((seam_codes % 2 == 1)[:, :, None, None], seams[:, :, ::-1], seams)
    corner_values = jnp.stack([edges[:, 0, 0], edges[:, 0, -1], edges[:, 2, -1], edges[:, 2, 0]], axis=1)
    corner_faces = neighbours[:, 4:]
    picked = corner_values[jnp.minimum(corner_faces, FACES - 1), codes[:, 4:]]
    picked = jnp.where((corner_faces < FACES)[:, :, None], picked, jnp.zeros_like(picked))
    return seams, picked


def surround(face_values, seams, corners):
    upper = jnp.concatenate([corners[0:1], seams[0], corners[1:2]], 0)
    lower = jnp.concatenate([corners[3:4], seams[2], corners[2:3]], 0)
    middle = jnp.concatenate([seams[3][:, None], face_values, seams[1][:, None]], 1)
    return jnp.concatenate([upper[None], middle, lower[None]], 0)


def convolve(padded, weight, bias):
    summed = lax.conv_general_dilated(padded, weight, (1, 1), "VALID", dimension_numbers=layout, preferred_element_type=jnp.float32)
    return jax.nn.gelu(summed + bias, approximate=False).astype(jnp.bfloat16)


def level(values, weight, bias, neighbours, codes):
    seams, corners = seam_parts(face_edges(values), neighbours, codes)

    def single(items):
        face_values, face_seams, face_corners = items
        return convolve(surround(face_values, face_seams, face_corners)[None], weight, bias)[0]

    return lax.map(single, (values, seams, corners))


def reference(field, conv1_w, conv1_b, conv2_w, conv2_b, down_w, down_b, neighbour_face, orientation):
    hidden = level(field, conv1_w, conv1_b, neighbour_face, orientation)
    skip = level(hidden, conv2_w, conv2_b, neighbour_face, orientation)

    def shrink(face_values):
        summed = lax.conv_general_dilated(face_values[None], down_w, (2, 2), "VALID", dimension_numbers=layout, preferred_element_type=jnp.float32)
        return (summed + down_b)[0].astype(jnp.bfloat16)

    coarse = lax.map(shrink, skip)
    return skip, coarse
```

```python
import functools, jax, jax.numpy as jnp
from jax import lax
from jax.experimental import pallas as pl
from jax.experimental.pallas import tpu as pltpu

COEF = (0.7978842854499817, 0.03633414953947067, -3.302673940197565e-05, -5.5273376347031444e-05, 3.974068931711372e-06, -1.3378310370626423e-07, 1.8139250101967264e-09)

def gelu(v):
    s = jnp.minimum(v * v, 64.0)
    p = COEF[-1] * s + COEF[-2]
    for k in COEF[-3::-1]:
        p = p * s + k
    h = 0.5 * v
    return h + h * jnp.tanh(p * v)

def build_w2(w_ref, w2):
    zero = jnp.zeros((128, 128), jnp.bfloat16)
    for t in range(4):
        for d in range(3):
            for p in range(2):
                w2[pl.ds(t*384+d*128, 128), pl.ds(p*128, 128)] = w_ref[t-p, d] if 0 <= t-p <= 2 else zero

def build_wd(wd_ref, wd):
    for d in range(2):
        for a in range(2):
            wd[pl.ds((d*2+a)*128, 128), :] = wd_ref[a, d]

def widen(v, left, right):
    n = v.shape[1]
    col = lax.broadcasted_iota(jnp.int32, v.shape, 1)
    a = jnp.where(col == 0, left[:, None, :], pltpu.roll(v, 1, 1))
    b = jnp.where(col == n-1, right[:, None, :], pltpu.roll(v, n-1, 1))
    return a.astype(jnp.bfloat16), b.astype(jnp.bfloat16)

def conv_kernel(down, PAIRS, *refs):
    if down:
        x, h, c, w_ref, b_ref, wd_ref, bd_ref, out, coarse, xc, w2, wd, g32 = refs
    else:
        x, h, c, w_ref, b_ref, out, xc, w2 = refs
    f = pl.program_id(0)
    @pl.when(f == 0)
    def _():
        build_w2(w_ref, w2)
        if down:
            build_wd(wd_ref, wd)
    f32 = jnp.float32
    for (src, row, cl, cr) in ((0, 0, 0, 1), (2, 65, 3, 2)):
        v = h[src, f]
        a, b = widen(v.astype(f32)[None], c[cl, pl.ds(f, 1)], c[cr, pl.ds(f, 1)])
        k = row
        xc[k//2, k%2, :, 0:128] = a[0]
        xc[k//2, k%2, :, 128:256] = v
        xc[k//2, k%2, :, 256:384] = b[0]
    def rows(g, _):
        v = x[0, pl.ds(8*g, 8)]
        left = h[3, f, pl.ds(pl.multiple_of(16*(g//2), 16), 16)].astype(f32)
        right = h[1, f, pl.ds(pl.multiple_of(16*(g//2), 16), 16)].astype(f32)
        odd = (g % 2) == 1
        left = jnp.where(odd, left[8:], left[:8])
        right = jnp.where(odd, right[8:], right[:8])
        a, b = widen(v.astype(f32), left, right)
        for i in range(8):
            k = 1 + i
            xc[4*g + k//2, k%2, :, 0:128] = a[i]
            xc[4*g + k//2, k%2, :, 128:256] = v[i]
            xc[4*g + k//2, k%2, :, 256:384] = b[i]
        return 0
    lax.fori_loop(0, 8, rows, 0)
    bias = jnp.concatenate([b_ref[...], b_ref[...]], axis=1)
    def chunk(g, _):
        lhs = jnp.concatenate([xc[pl.ds(PAIRS*g + t//2, PAIRS), t % 2].reshape(PAIRS*64, 384) for t in range(4)], axis=1)
        acc = jnp.dot(lhs, w2[...], preferred_element_type=f32)
        o = gelu(acc + bias)
        ob = o.astype(jnp.bfloat16)
        for p in range(2):
            out[0, pl.ds(PAIRS*g, PAIRS), p] = ob[:, p*128:(p+1)*128].reshape(PAIRS, 64, 128)
        if down:
            g32[0] = o[:, 0:128]
            g32[1] = o[:, 128:256]
            parts = [g32[a, pl.ds(d, PAIRS*32, stride=2), :] for d in range(2) for a in range(2)]
            q = jnp.concatenate(parts, axis=1).astype(jnp.bfloat16)
            cc = jnp.dot(q, wd[...], preferred_element_type=f32) + bd_ref[...]
            coarse[0, pl.ds(PAIRS*g, PAIRS)] = cc.astype(jnp.bfloat16).reshape(PAIRS, 32, 256)
        return 0
    lax.fori_loop(0, 32//PAIRS, chunk, 0)

def conv(x, h, c, w, b, wd=None, bd=None, PAIRS=8):
    down = wd is not None
    full = lambda shape: pl.BlockSpec(shape, lambda f: (0,)*len(shape))
    in_specs = [pl.BlockSpec((1,64,64,128), lambda f: (f,0,0,0)), full((4,3,64,128)), full((4,8,128)), full((3,3,128,128)), full((1,128))]
    args = [x, h, c, w, b.reshape(1,128)]
    out_shape = [jax.ShapeDtypeStruct((3,32,2,64,128), jnp.bfloat16)]
    out_specs = [pl.BlockSpec((1,32,2,64,128), lambda f: (f,0,0,0,0))]
    scratch = [pltpu.VMEM((33,2,64,384), jnp.bfloat16), pltpu.VMEM((1536,256), jnp.bfloat16)]
    if down:
        in_specs += [full((2,2,128,256)), full((1,256))]
        args += [wd, bd.reshape(1,256)]
        out_shape.append(jax.ShapeDtypeStruct((3,32,32,256), jnp.bfloat16))
        out_specs.append(pl.BlockSpec((1,32,32,256), lambda f: (f,0,0,0)))
        scratch += [pltpu.VMEM((512,256), jnp.bfloat16), pltpu.VMEM((2,PAIRS*64,128), jnp.float32)]
    r = pl.pallas_call(
        functools.partial(conv_kernel, down, PAIRS), grid=(3,), in_specs=in_specs, out_specs=out_specs,
        out_shape=out_shape, scratch_shapes=scratch,
        compiler_params=pltpu.CompilerParams(vmem_limit_bytes=50*2**20, dimension_semantics=("arbitrary",)),
    )(*args)
    return [r[0].reshape(3,64,64,128)] + list(r[1:])


MESH = pl.DeviceIdType.MESH
F32, BF16 = jnp.float32, jnp.bfloat16


def place():
    face, row, col = lax.axis_index("face"), lax.axis_index("row"), lax.axis_index("col")
    rows, cols = lax.axis_size("row"), lax.axis_size("col")
    top, bottom, left, right = row == 0, row == rows - 1, col == 0, col == cols - 1
    return face, row, col, top, bottom, left, right


class Exchange:
    def __init__(self, lines, halo, cells, nf, ori, pool, send_b, recv_b, tip_s, tip_r, end_s, end_r, sems):
        self.lines, self.halo, self.cells, self.nf, self.ori = lines, halo, cells, nf, ori
        self.pool, self.send_b, self.recv_b = pool, send_b, recv_b
        self.tip_s, self.tip_r, self.end_s, self.end_r = tip_s, tip_r, end_s, end_r
        (self.hs, self.hr, self.as_, self.ar, self.bs, self.br, self.ts, self.tr, self.es, self.er) = sems
        face, row, col, top, bottom, left, right = place()
        self.face, self.row, self.col = face, row, col
        self.top, self.bottom, self.left, self.right = top, bottom, left, right
        self.has_h = jnp.logical_or(top, bottom)
        self.has_v = jnp.logical_or(left, right)
        self.corner = jnp.logical_and(self.has_h, self.has_v)
        self.rim = jnp.logical_or(self.has_h, self.has_v)
        self.edge_h = jnp.where(top, 0, 2)
        self.edge_v = jnp.where(left, 3, 1)
        self.slot_h = self.edge_h * 2 + jnp.where(col >= 4, 1, 0)
        self.slot_v = self.edge_v * 2 + jnp.where(row >= 4, 1, 0)
        self.kind = ((self.has_h, self.edge_h, self.slot_h, col), (self.has_v, self.edge_v, self.slot_v, row))
        self.tip = jnp.where(top, jnp.where(left, 0, 1), jnp.where(left, 3, 2))
        not_ = jnp.logical_not
        self.beside = (
            (not_(top), (face, row - 1, col), 0, 2),
            (not_(bottom), (face, row + 1, col), 2, 0),
            (not_(left), (face, row, col - 1), 3, 1),
            (not_(right), (face, row, col + 1), 1, 3),
        )

    def classmates(self, which):
        has, edge, slot, seg = self.kind[which]
        low = jnp.where(seg >= 4, 7 - seg, seg)
        for q in range(8):
            s = low if q % 2 == 0 else 7 - low
            tr, tc = ((0, s), (s, 7), (7, s), (s, 0))[q // 2]
            other = jnp.logical_or(self.row != tr, self.col != tc)
            ok = jnp.logical_and(has, other)
            if q not in (0, 1, 4, 5):
                ok = jnp.logical_and(ok, low > 0)
            yield q, ok, (self.face, tr, tc)

    def across(self):
        for d in (1, 2, 3):
            yield d - 1, (lax.rem(self.face + d, 4), self.row, self.col)

    def greet(self):
        barrier = pltpu.get_barrier_semaphore()
        partners = [(ok, dev) for ok, dev, _, _ in self.beside]
        partners += [(self.rim, dev) for _, dev in self.across()]
        partners += [(ok, dev) for which in (0, 1) for _, ok, dev in self.classmates(which)]
        total = 0
        for ok, dev in partners:
            @pl.when(ok)
            def _(dev=dev):
                pl.semaphore_signal(barrier, inc=1, device_id=dev, device_id_type=MESH)
            total = total + jnp.where(ok, 1, 0)
        pl.semaphore_wait(barrier, total)

    def copies_beside(self):
        for ok, dev, line, rim in self.beside:
            yield ok, rim, pltpu.make_async_remote_copy(
                self.lines.at[line], self.halo.at[rim], self.hs.at[line], self.hr.at[rim],
                device_id=dev, device_id_type=MESH)

    def copies_class(self):
        for which in (0, 1):
            has, edge, slot, seg = self.kind[which]
            for q, ok, dev in self.classmates(which):
                yield ok, pltpu.make_async_remote_copy(
                    self.lines.at[edge], self.pool.at[slot], self.as_.at[which, q], self.ar.at[slot],
                    device_id=dev, device_id_type=MESH)

    def start_a(self):
        for ok, copy in self.copies_class():
            @pl.when(ok)
            def _(copy=copy):
                copy.start()
        for ok, _, copy in self.copies_beside():
            @pl.when(ok)
            def _(copy=copy):
                copy.start()
        for has, edge, slot, seg in self.kind:
            @pl.when(has)
            def _(edge=edge, slot=slot):
                self.pool[slot] = self.lines[edge]

    def copies_b(self, which):
        for d, dev in self.across():
            yield d, dev, pltpu.make_async_remote_copy(
                self.send_b.at[which, d], self.recv_b.at[which, self.face], self.bs.at[which, d],
                self.br.at[which, self.face], device_id=dev, device_id_type=MESH)

    def copies_tip(self):
        for d, dev in self.across():
            yield d, dev, pltpu.make_async_remote_copy(
                self.tip_s.at[d], self.tip_r.at[self.face], self.ts.at[d], self.tr.at[self.face],
                device_id=dev, device_id_type=MESH)

    def picked(self, which, face, i):
        has, edge, slot, seg = self.kind[which]
        n, o = self.nf[face * 3 + i, edge], self.ori[face * 3 + i, edge]
        side, turned = lax.div(o, 2), lax.rem(o, 2)
        s = jnp.where(turned == 1, 7 - seg, seg)
        return self.pool[side * 2 + jnp.where(s >= 4, 1, 0), lax.rem(n, 3)]

    def picked_tip(self, face, i):
        n, k = jnp.minimum(self.nf[face * 3 + i, 4 + self.tip], 11), self.ori[face * 3 + i, 4 + self.tip]
        line = self.pool[jnp.where(k == 2, 5, jnp.where(k == 3, 4, k)), lax.rem(n, 3)].astype(F32)
        last = jnp.logical_or(k == 1, k == 2)
        return jnp.where(last, line[63:64], line[0:1])

    def stage_b(self):
        @pl.when(self.rim)
        def _():
            for q in range(8):
                own = jnp.logical_or(jnp.logical_and(self.has_h, self.slot_h == q), jnp.logical_and(self.has_v, self.slot_v == q))
                @pl.when(jnp.logical_not(own))
                def _(q=q):
                    self.recv_wait(self.pool.at[q], self.ar.at[q])
            for which in (0, 1):
                has = self.kind[which][0]
                @pl.when(has)
                def _(which=which):
                    for d, dev, copy in self.copies_b(which):
                        for i in range(3):
                            self.send_b[which, d, i] = self.picked(which, dev[0], i)
                        copy.start()
                    for i in range(3):
                        self.recv_b[which, self.face, i] = self.picked(which, self.face, i)
            @pl.when(self.corner)
            def _():
                for d, dev, copy in self.copies_tip():
                    for i in range(3):
                        self.tip_s[d, pl.ds(i, 1)] = self.picked_tip(dev[0], i)
                    copy.start()
                for i in range(3):
                    self.tip_r[self.face, pl.ds(i, 1)] = self.picked_tip(self.face, i)

    def recv_wait(self, dst, sem):
        pltpu.make_async_copy(dst, dst, sem).wait()

    def stage_c(self):
        i0 = lax.broadcasted_iota(jnp.int32, (64, 64), 0)
        i1 = lax.broadcasted_iota(jnp.int32, (64, 64), 1)
        for which in (0, 1):
            @pl.when(self.kind[which][0])
            def _(which=which):
                for d in (1, 2, 3):
                    other = lax.rem(self.face + d, 4)
                    self.recv_wait(self.recv_b.at[which, other], self.br.at[which, other])
        for which in (0, 1):
            has, edge, slot, seg = self.kind[which]
            @pl.when(has)
            def _(which=which, edge=edge):
                for i in range(3):
                    n, o = self.nf[self.face * 3 + i, edge], self.ori[self.face * 3 + i, edge]
                    line = self.recv_b[which, lax.div(n, 3), i]
                    turned = lax.rem(o, 2) == 1
                    order = jnp.where(i1 == jnp.where(turned, 63 - i0, i0), 1.0, 0.0).astype(BF16)
                    self.halo[edge, i] = jnp.dot(order, line, preferred_element_type=F32).astype(BF16)
        for ok, rim, copy in self.copies_beside():
            side = {2: 0, 0: 2, 1: 3, 3: 1}[rim]
            @pl.when(ok)
            def _(side=side):
                self.recv_wait(self.halo.at[side], self.hr.at[side])

    def copies_ends(self):
        for slot, land in ((2, 3), (3, 2), (0, 1), (1, 0)):
            ok, dev = {2: self.beside[0], 3: self.beside[1], 0: self.beside[2], 1: self.beside[3]}[slot][:2]
            if slot >= 2:
                ok = jnp.logical_and(ok, self.has_v)
            yield slot, ok, pltpu.make_async_remote_copy(
                self.end_s.at[slot], self.end_r.at[land], self.es.at[slot], self.er.at[land],
                device_id=dev, device_id_type=MESH)

    def start_d(self):
        for slot, ok, copy in self.copies_ends():
            @pl.when(ok)
            def _(slot=slot, copy=copy):
                row = 63 if slot in (1, 3) else 0
                for i in range(3):
                    if slot < 2:
                        self.end_s[slot, pl.ds(i, 1)] = self.halo[0, i].astype(F32)[row:row + 1]
                        self.end_s[slot, pl.ds(8 + i, 1)] = self.halo[2, i].astype(F32)[row:row + 1]
                    else:
                        self.end_s[slot, pl.ds(i, 1)] = self.halo[self.edge_v, i].astype(F32)[row:row + 1]
                copy.start()

    def finish(self):
        for slot, ok, copy in self.copies_ends():
            @pl.when(ok)
            def _(slot=slot):
                self.recv_wait(self.end_r.at[slot], self.er.at[slot])
        @pl.when(self.corner)
        def _():
            for d in (1, 2, 3):
                other = lax.rem(self.face + d, 4)
                self.recv_wait(self.tip_r.at[other], self.tr.at[other])
            for i in range(3):
                n = self.nf[self.face * 3 + i, 4 + self.tip]
                got = self.tip_r[lax.div(jnp.minimum(n, 11), 3), pl.ds(i, 1)]
                self.cells[self.tip, pl.ds(i, 1)] = jnp.where(n < 12, got, 0.0)
        not_, and_ = jnp.logical_not, jnp.logical_and
        for cell, flat, part, flat_slot, upright, up_slot in (
            (0, not_(self.left), 0, 0, not_(self.top), 2),
            (1, not_(self.right), 0, 1, not_(self.top), 2),
            (2, not_(self.right), 8, 1, not_(self.bottom), 3),
            (3, not_(self.left), 8, 0, not_(self.bottom), 3),
        ):
            @pl.when(flat)
            def _(cell=cell, part=part, flat_slot=flat_slot):
                self.cells[cell] = self.end_r[flat_slot, pl.ds(part, 8)]
            @pl.when(and_(not_(flat), upright))
            def _(cell=cell, up_slot=up_slot):
                self.cells[cell] = self.end_r[up_slot, pl.ds(0, 8)]

    def wait_sends(self):
        for ok, _, copy in self.copies_beside():
            @pl.when(ok)
            def _(copy=copy):
                copy.wait_send()
        for ok, copy in self.copies_class():
            @pl.when(ok)
            def _(copy=copy):
                copy.wait_send()
        for which in (0, 1):
            @pl.when(self.kind[which][0])
            def _(which=which):
                for _, _, copy in self.copies_b(which):
                    copy.wait_send()
        @pl.when(self.corner)
        def _():
            for _, _, copy in self.copies_tip():
                copy.wait_send()
        for _, ok, copy in self.copies_ends():
            @pl.when(ok)
            def _(copy=copy):
                copy.wait_send()


EXCHANGE_SCRATCH = [
    pltpu.VMEM((8, 3, 64, 128), BF16),
    pltpu.VMEM((2, 3, 3, 64, 128), BF16),
    pltpu.VMEM((2, 4, 3, 64, 128), BF16),
    pltpu.VMEM((3, 8, 128), F32),
    pltpu.VMEM((4, 8, 128), F32),
    pltpu.VMEM((4, 16, 128), F32),
    pltpu.VMEM((4, 16, 128), F32),
    pltpu.SemaphoreType.DMA((4,)), pltpu.SemaphoreType.DMA((4,)),
    pltpu.SemaphoreType.DMA((2, 8)), pltpu.SemaphoreType.DMA((8,)),
    pltpu.SemaphoreType.DMA((2, 3)), pltpu.SemaphoreType.DMA((2, 4)),
    pltpu.SemaphoreType.DMA((3,)), pltpu.SemaphoreType.DMA((4,)),
    pltpu.SemaphoreType.DMA((4,)), pltpu.SemaphoreType.DMA((4,)),
]


def exchange_kernel(x, nf, ori, h_out, c_out, lines, sides, halo, load, *rest):
    bufs, sems = rest[:7], rest[7:]
    ex = Exchange(lines, halo, c_out, nf, ori, *bufs, sems)
    moves = [pltpu.make_async_copy(x.at[:, 0], lines.at[0], load.at[0]),
             pltpu.make_async_copy(x.at[:, 63], lines.at[2], load.at[1]),
             pltpu.make_async_copy(x.at[:, :, pl.ds(0, 16)], sides.at[0], load.at[2]),
             pltpu.make_async_copy(x.at[:, :, pl.ds(48, 16)], sides.at[1], load.at[3])]
    for m in moves:
        m.start()
    for k in range(4):
        ex.end_s[k] = jnp.zeros((16, 128), F32)
        c_out[k] = jnp.zeros((8, 128), F32)
    for k in range(3):
        ex.tip_s[k] = jnp.zeros((8, 128), F32)
    ex.greet()
    for m in moves:
        m.wait()
    for i in range(3):
        lines[3, i] = sides[0, i].astype(F32)[:, 0].astype(BF16)
        lines[1, i] = sides[1, i].astype(F32)[:, 15].astype(BF16)
    ex.start_a()
    ex.stage_b()
    ex.stage_c()
    ex.start_d()
    ex.finish()
    h_out[...] = halo[...]
    ex.wait_sends()


def exchange(x, nf, ori, number):
    vm = pl.BlockSpec(memory_space=pltpu.VMEM)
    sm = pl.BlockSpec(memory_space=pltpu.SMEM)
    return pl.pallas_call(
        exchange_kernel,
        in_specs=[pl.BlockSpec(memory_space=pl.ANY), sm, sm],
        out_specs=[vm, vm],
        out_shape=[jax.ShapeDtypeStruct((4, 3, 64, 128), BF16), jax.ShapeDtypeStruct((4, 8, 128), F32)],
        scratch_shapes=[pltpu.VMEM((4, 3, 64, 128), BF16), pltpu.VMEM((2, 3, 64, 16, 128), BF16),
                        pltpu.VMEM((4, 3, 64, 128), BF16), pltpu.SemaphoreType.DMA((4,))] + EXCHANGE_SCRATCH,
        compiler_params=pltpu.CompilerParams(collective_id=number, has_side_effects=True, vmem_limit_bytes=40 * 2**20),
    )(x, nf, ori)


def per_device(field, conv1_w, conv1_b, conv2_w, conv2_b, down_w, down_b, neighbour_face, orientation):
    h, c = exchange(field, neighbour_face, orientation, 0)
    hidden, = conv(field, h, c, conv1_w, conv1_b, PAIRS=16)
    h, c = exchange(hidden, neighbour_face, orientation, 1)
    skip, coarse = conv(hidden, h, c, conv2_w, conv2_b, down_w, down_b, PAIRS=16)
    return skip, coarse


def solution(mesh):
    from jax.sharding import PartitionSpec as P
    return jax.shard_map(
        per_device, mesh=mesh,
        in_specs=(P("face", "row", "col", None), P(), P(), P(), P(), P(), P(), P(), P()),
        out_specs=(P("face", "row", "col", None), P("face", "row", "col", None)),
        check_vma=False,
    )
```

```python
import jax
import jax.numpy as jnp
from jax import lax
from jax.experimental import pallas as pl
from jax.experimental.pallas import tpu as pltpu
from jax.sharding import PartitionSpec as P

MESH = pl.DeviceIdType.MESH
F32, BF16 = jnp.float32, jnp.bfloat16
PAIRS = 16

COEF = (0.7978842854499817, 0.03633414953947067, -3.302673940197565e-05, -5.5273376347031444e-05, 3.974068931711372e-06, -1.3378310370626423e-07, 1.8139250101967264e-09)

def gelu(v):
    s = jnp.minimum(v * v, 64.0)
    p = COEF[-1] * s + COEF[-2]
    for k in COEF[-3::-1]:
        p = p * s + k
    h = 0.5 * v
    return h + h * jnp.tanh(p * v)

def build_wd(wd_ref, wd):
    for d in range(2):
        for a in range(2):
            wd[pl.ds((d*2+a)*128, 128), :] = wd_ref[a, d]

def loop(count, body):
    def step(k, _):
        body(k)
        return 0

    lax.fori_loop(0, count, step, 0)


class Exchange:
    def __init__(self, lines, halo, cells, nf, ori, pool, send_b, recv_b, tip_s, tip_r, end_s, end_r, sems, seen):
        self.lines, self.halo, self.cells, self.nf, self.ori = lines, halo, cells, nf, ori
        self.pool, self.send_b, self.recv_b = pool, send_b, recv_b
        self.tip_s, self.tip_r, self.end_s, self.end_r = tip_s, tip_r, end_s, end_r
        (self.hs, self.hr, self.as_, self.ar, self.bs, self.br, self.ts, self.tr, self.es, self.er) = sems
        self.pool_w, self.recv_w, self.tip_w = seen
        self.face, self.row, self.col = lax.axis_index("face"), lax.axis_index("row"), lax.axis_index("col")
        self.top, self.bottom = self.row == 0, self.row == 7
        self.left, self.right = self.col == 0, self.col == 7
        self.has_h = jnp.logical_or(self.top, self.bottom)
        self.has_v = jnp.logical_or(self.left, self.right)
        self.corner = jnp.logical_and(self.has_h, self.has_v)
        self.rim = jnp.logical_or(self.has_h, self.has_v)
        self.edge_h = jnp.where(self.top, 0, 2)
        self.edge_v = jnp.where(self.left, 3, 1)
        self.tip = jnp.where(self.top, jnp.where(self.left, 0, 1), jnp.where(self.left, 3, 2))

    def own(self, which):
        flat = which == 0
        has = jnp.logical_or(jnp.logical_and(flat, self.has_h), jnp.logical_and(jnp.logical_not(flat), self.has_v))
        edge = jnp.where(flat, self.edge_h, self.edge_v)
        seg = jnp.where(flat, self.col, self.row)
        return has, edge, seg, edge * 2 + jnp.where(seg >= 4, 1, 0)

    def beside(self, side):
        r = self.row + jnp.where(side == 0, -1, jnp.where(side == 2, 1, 0))
        c = self.col + jnp.where(side == 1, 1, jnp.where(side == 3, -1, 0))
        ok = jnp.logical_and(jnp.logical_and(r >= 0, r <= 7), jnp.logical_and(c >= 0, c <= 7))
        return ok, (self.face, r, c)

    def classmate(self, k):
        which, q = lax.div(k, 8), lax.rem(k, 8)
        has, edge, seg, slot = self.own(which)
        low = jnp.where(seg >= 4, 7 - seg, seg)
        s = jnp.where(lax.rem(q, 2) == 0, low, 7 - low)
        e = lax.div(q, 2)
        r = jnp.where(e == 0, 0, jnp.where(e == 2, 7, s))
        c = jnp.where(e == 1, 7, jnp.where(e == 3, 0, s))
        other = jnp.logical_or(r != self.row, c != self.col)
        once = jnp.logical_or(low > 0, lax.rem(q, 4) < 2)
        return which, q, edge, slot, jnp.logical_and(has, jnp.logical_and(other, once)), (self.face, r, c)

    def across(self, d):
        return (lax.rem(self.face + d, 4), self.row, self.col)

    def greet(self):
        barrier = pltpu.get_barrier_semaphore()

        def meet(ok, dev):
            @pl.when(ok)
            def _():
                pl.semaphore_signal(barrier, inc=1, device_id=dev, device_id_type=MESH)

        loop(4, lambda k: meet(*self.beside(k)))
        loop(16, lambda k: meet(*self.classmate(k)[4:]))
        loop(3, lambda k: meet(self.rim, self.across(k + 1)))

    def greeted(self):
        barrier = pltpu.get_barrier_semaphore()

        near = sum(jnp.where(end, 0, 1) for end in (self.top, self.bottom, self.left, self.right))
        far = jnp.where(self.corner, 9, jnp.where(self.rim, 10, 0))
        pl.semaphore_wait(barrier, near + far)

    def copy_beside(self, side):
        ok, dev = self.beside(side)
        there = lax.rem(side + 2, 4)
        return ok, pltpu.make_async_remote_copy(
            self.lines.at[side], self.halo.at[there], self.hs.at[side], self.hr.at[there],
            device_id=dev, device_id_type=MESH)

    def copy_class(self, k):
        which, q, edge, slot, ok, dev = self.classmate(k)
        return ok, pltpu.make_async_remote_copy(
            self.lines.at[edge], self.pool.at[slot], self.as_.at[which, q], self.ar.at[slot],
            device_id=dev, device_id_type=MESH)

    def copy_across(self, k):
        which, d = lax.div(k, 3), lax.rem(k, 3) + 1
        return self.own(which)[0], pltpu.make_async_remote_copy(
            self.send_b.at[which, d], self.recv_b.at[which, self.face], self.bs.at[which, d],
            self.br.at[which, self.face], device_id=self.across(d), device_id_type=MESH)

    def copy_tip(self, k):
        d = k + 1
        return self.corner, pltpu.make_async_remote_copy(
            self.tip_s.at[d], self.tip_r.at[self.face], self.ts.at[d], self.tr.at[self.face],
            device_id=self.across(d), device_id_type=MESH)

    def copy_end(self, side):
        ok, dev = self.beside(side)
        there = lax.rem(side + 2, 4)
        ok = jnp.logical_and(ok, jnp.logical_or(lax.rem(side, 2) == 1, self.has_v))
        return ok, pltpu.make_async_remote_copy(
            self.end_s.at[side], self.end_r.at[there], self.es.at[side], self.er.at[there],
            device_id=dev, device_id_type=MESH)

    @staticmethod
    def start(pair):
        ok, copy = pair

        @pl.when(ok)
        def _():
            copy.start()

    @staticmethod
    def sent(pair):
        ok, copy = pair

        @pl.when(ok)
        def _():
            copy.wait_send()

    @staticmethod
    def landed(ok, dst, sem):
        @pl.when(ok)
        def _():
            pltpu.make_async_copy(dst, dst, sem).wait()

    def start_a(self):
        loop(16, lambda k: self.start(self.copy_class(k)))
        loop(4, lambda k: self.start(self.copy_beside(k)))

        def keep(which):
            has, edge, seg, slot = self.own(which)

            @pl.when(has)
            def _():
                self.pool[slot] = self.lines[edge]

        loop(2, keep)

    def picked(self, which, face, i):
        has, edge, seg, slot = self.own(which)
        n, o = self.nf[edge, face * 3 + i], self.ori[edge, face * 3 + i]
        side, turned = lax.div(o, 2), lax.rem(o, 2)
        s = jnp.where(turned == 1, 7 - seg, seg)
        return self.pool_w[side * 2 + jnp.where(s >= 4, 1, 0), lax.rem(n, 3)]

    def picked_tip(self, face, i):
        n, k = jnp.minimum(self.nf[4 + self.tip, face * 3 + i], 11), self.ori[4 + self.tip, face * 3 + i]
        line = self.pool_w[jnp.where(k == 2, 5, jnp.where(k == 3, 4, k)), lax.rem(n, 3)].astype(F32)
        return jnp.where(jnp.logical_or(k == 1, k == 2), line[63:64], line[0:1])

    def stage_b(self):
        @pl.when(self.rim)
        def _():
            slot_h, slot_v = self.own(0)[3], self.own(1)[3]

            def arrived(q):
                mine = jnp.logical_or(
                    jnp.logical_and(self.has_h, slot_h == q), jnp.logical_and(self.has_v, slot_v == q))
                self.landed(jnp.logical_not(mine), self.pool.at[q], self.ar.at[q])

            loop(8, arrived)

            def take(q):
                self.pool_w[q] = self.pool[q]

            loop(8, take)

            def pick(k):
                which, d = lax.div(k, 4), lax.rem(k + 1, 4)

                @pl.when(self.own(which)[0])
                def _():
                    for i in range(3):
                        self.send_b[which, d, i] = self.picked(which, self.across(d)[0], i)

                    @pl.when(d > 0)
                    def _():
                        self.copy_across(which * 3 + jnp.maximum(d - 1, 0))[1].start()

            loop(8, pick)

            @pl.when(self.corner)
            def _():
                def tips(k):
                    d = lax.rem(k + 1, 4)
                    for i in range(3):
                        self.tip_s[d, pl.ds(i, 1)] = self.picked_tip(self.across(d)[0], i)

                    @pl.when(d > 0)
                    def _():
                        self.copy_tip(jnp.maximum(d - 1, 0))[1].start()

                loop(4, tips)

    def stage_c(self):
        def arrived(k):
            which, other = lax.div(k, 3), lax.rem(self.face + 1 + lax.rem(k, 3), 4)
            self.landed(self.own(which)[0], self.recv_b.at[which, other], self.br.at[which, other])

        loop(6, arrived)

        def take(k):
            which, group = lax.div(k, 4), lax.rem(k, 4)
            has = self.own(which)[0]

            @pl.when(jnp.logical_and(has, group != self.face))
            def _():
                self.recv_w[which, group] = self.recv_b[which, group]

        loop(8, take)
        i0 = lax.broadcasted_iota(jnp.int32, (64, 64), 0)
        i1 = lax.broadcasted_iota(jnp.int32, (64, 64), 1)

        def turn(k):
            which, i = lax.div(k, 3), lax.rem(k, 3)
            has, edge, seg, slot = self.own(which)

            @pl.when(has)
            def _():
                n, o = self.nf[edge, self.face * 3 + i], self.ori[edge, self.face * 3 + i]
                group = lax.div(n, 3)
                order = jnp.where(i1 == jnp.where(lax.rem(o, 2) == 1, 63 - i0, i0), 1.0, 0.0).astype(BF16)
                near = jnp.dot(order, self.send_b[which, 0, i], preferred_element_type=F32)
                far = jnp.dot(order, self.recv_w[which, group, i], preferred_element_type=F32)
                self.halo[edge, i] = jnp.where(group == self.face, near, far).astype(BF16)

        loop(6, turn)
        loop(4, lambda k: self.landed(self.beside(k)[0], self.halo.at[k], self.hr.at[k]))

    def start_d(self):
        def ends(side):
            last = jnp.logical_or(side == 1, side == 2)
            for i in range(3):
                for part, line in ((0, jnp.where(lax.rem(side, 2) == 1, 0, self.edge_v)), (8, 2)):
                    v = self.halo[line, i].astype(F32)
                    self.end_s[side, pl.ds(part + i, 1)] = jnp.where(last, v[63:64], v[0:1])

            self.start(self.copy_end(side))

        loop(4, ends)

    def finish(self):
        loop(4, lambda k: self.landed(self.copy_end_ok(k), self.end_r.at[k], self.er.at[k]))

        @pl.when(self.corner)
        def _():
            def arrived(k):
                other = lax.rem(self.face + 1 + k, 4)
                self.landed(self.corner, self.tip_r.at[other], self.tr.at[other])

            loop(3, arrived)
            self.tip_w[...] = self.tip_r[...]
            for i in range(3):
                n = self.nf[4 + self.tip, self.face * 3 + i]
                group = lax.div(jnp.minimum(n, 11), 3)
                got = jnp.where(group == self.face, self.tip_s[0, pl.ds(i, 1)], self.tip_w[group, pl.ds(i, 1)])
                self.cells[self.tip, pl.ds(i, 1)] = jnp.where(n < 12, got, 0.0)

        not_, and_ = jnp.logical_not, jnp.logical_and
        for cell, flat, part, flat_side, upright, up_side in (
            (0, not_(self.left), 0, 3, not_(self.top), 0),
            (1, not_(self.right), 0, 1, not_(self.top), 0),
            (2, not_(self.right), 8, 1, not_(self.bottom), 2),
            (3, not_(self.left), 8, 3, not_(self.bottom), 2),
        ):
            @pl.when(flat)
            def _(cell=cell, part=part, flat_side=flat_side):
                self.cells[cell] = self.end_r[flat_side, pl.ds(part, 8)]

            @pl.when(and_(not_(flat), upright))
            def _(cell=cell, up_side=up_side):
                self.cells[cell] = self.end_r[up_side, pl.ds(0, 8)]

    def copy_end_ok(self, side):
        ok, dev = self.beside(side)
        return jnp.logical_and(ok, jnp.logical_or(lax.rem(side, 2) == 1, self.has_v))

    def wait_sends(self):
        loop(4, lambda k: self.sent(self.copy_beside(k)))
        loop(16, lambda k: self.sent(self.copy_class(k)))
        loop(6, lambda k: self.sent(self.copy_across(k)))
        loop(3, lambda k: self.sent(self.copy_tip(k)))
        loop(4, lambda k: self.sent(self.copy_end(k)))


EXCHANGE_SCRATCH = [
    pltpu.VMEM((2, 8, 3, 64, 128), BF16),
    pltpu.VMEM((2, 2, 4, 3, 64, 128), BF16),
    pltpu.VMEM((2, 2, 4, 3, 64, 128), BF16),
    pltpu.VMEM((2, 4, 8, 128), F32),
    pltpu.VMEM((2, 4, 8, 128), F32),
    pltpu.VMEM((2, 4, 16, 128), F32),
    pltpu.VMEM((2, 4, 16, 128), F32),
    pltpu.VMEM((8, 3, 64, 128), BF16), pltpu.VMEM((2, 4, 3, 64, 128), BF16), pltpu.VMEM((4, 8, 128), F32),
    pltpu.SemaphoreType.DMA((2, 4)), pltpu.SemaphoreType.DMA((2, 4)),
    pltpu.SemaphoreType.DMA((2, 2, 8)), pltpu.SemaphoreType.DMA((2, 8)),
    pltpu.SemaphoreType.DMA((2, 2, 4)), pltpu.SemaphoreType.DMA((2, 2, 4)),
    pltpu.SemaphoreType.DMA((2, 4)), pltpu.SemaphoreType.DMA((2, 4)),
    pltpu.SemaphoreType.DMA((2, 4)), pltpu.SemaphoreType.DMA((2, 4)),
]


def widen(w, out):
    out[...] = jnp.zeros(out.shape, BF16)
    for d in range(3):
        for p in range(2):
            for a in range(3):
                out[pl.ds((a + p) * 384 + d * 128, 128), pl.ds(p * 128, 128)] = w[a, d]


def build(f, img, xc, edges):
    col = lax.broadcasted_iota(jnp.int32, (8, 8, 128), 1)

    def rows(g):
        v = img[f, pl.ds(4 * g, 4)].reshape(8, 64, 128)
        wide = v.astype(F32)
        at = pl.ds(pl.multiple_of(8 * g, 8), 8)
        first = jnp.where(col == 0, edges[0, f, at][:, None, :], wide[:, 0:8])
        last = jnp.where(col == 7, edges[1, f, at][:, None, :], wide[:, 56:64])
        wide = jnp.concatenate([first, wide[:, 8:56], last], axis=1)
        parts = [pltpu.roll(wide, 1, 1).astype(BF16), wide.astype(BF16), pltpu.roll(wide, 63, 1).astype(BF16)]
        for i in range(8):
            k = 1 + i
            for d in range(3):
                xc[f, 4 * g + k // 2, k % 2, :, d * 128:(d + 1) * 128] = parts[d][i]

    loop(8, rows)


def inner(f, xc, w2, bias, img):
    def chunk(g):
        lhs = jnp.concatenate(
            [xc[f, pl.ds(PAIRS * g + t // 2, PAIRS), t % 2].reshape(PAIRS * 64, 384) for t in range(4)], axis=1)
        o = gelu(jnp.dot(lhs, w2[...], preferred_element_type=F32) + bias).astype(BF16)
        for p in range(2):
            img[f, pl.ds(PAIRS * g, PAIRS), p] = o[:, p * 128:(p + 1) * 128].reshape(PAIRS, 64, 128)

    loop(32 // PAIRS, chunk)


def ring(f, halo, cells, xc, cols, g, rl, w, bias, out, edges):
    for e, r in ((0, ((0, 1), (1, 0))), (2, ((31, 1), (32, 0)))):
        at = pl.ds(e * 64, 64)
        mid = halo[e, f]
        wide = mid.astype(F32)
        parts = (pltpu.roll(wide, 1, 0).astype(BF16), mid, pltpu.roll(wide, 63, 0).astype(BF16))
        h0, x0 = (0, 384) if e == 0 else (768, 0)
        for d in range(3):
            rl[at, pl.ds(h0 + d * 128, 128)] = parts[d]
        for k in range(2):
            rl[at, pl.ds(x0 + k * 384, 384)] = xc[f, r[k][0], r[k][1]]
    upper, lower = halo[0, f].astype(F32), halo[2, f].astype(F32)
    for side, e, lanes, px in ((0, 3, (0, 1, 2), 0), (1, 1, (2, 0, 1), 62)):
        rim, c0, c1 = [pl.ds(k * 128, 128) for k in lanes]
        mid = pl.ds(1, 64)
        g[side, mid, rim] = halo[e, f].astype(F32)
        g[side, mid, c0] = cols[2 * side, f]
        g[side, mid, c1] = cols[2 * side + 1, f]
        for at, line, cell in ((0, upper, (0, 1)[side]), (65, lower, (3, 2)[side])):
            g[side, at:at + 1, rim] = cells[cell, pl.ds(f, 1)]
            g[side, at:at + 1, c0] = line[px:px + 1]
            g[side, at:at + 1, c1] = line[px + 1:px + 2]
        for a in range(3):
            rl[pl.ds(e * 64, 64), pl.ds(a * 384, 384)] = g[side, pl.ds(a, 64)].astype(BF16)
    o = gelu(jnp.dot(rl[...], w, preferred_element_type=F32) + bias)
    row = lax.broadcasted_iota(jnp.int32, (64, 128), 0)
    left, right = o[192:256], o[64:128]
    out[3, f] = left.astype(BF16)
    out[1, f] = right.astype(BF16)
    edges[0, f] = left
    edges[1, f] = right
    for e, k in ((0, 0), (2, 63)):
        line = jnp.where(row == 0, left[k:k + 1], jnp.where(row == 63, right[k:k + 1], o[e * 64:(e + 1) * 64]))
        out[e, f] = line.astype(BF16)


def main_kernel(x, nf_in, ori_in, w1, b1, w2, b2, skip, ring_out,
                img, nf, ori, xc, wv, bv, wide, lines, halo, cells, cols, edges, g, rl, load, store, *rest):
    bufs, seen, sems = rest[:7], rest[7:10], rest[10:]

    def exchange(layer):
        return Exchange(lines.at[layer], halo.at[layer], cells.at[layer], nf, ori,
                        *[b.at[layer] for b in bufs], [s.at[layer] for s in sems], seen)

    moves = [pltpu.make_async_copy(src, dst, load.at[k]) for k, (src, dst) in enumerate((
        (x, img), (nf_in, nf), (ori_in, ori), (w1, wv.at[0]), (w2, wv.at[1]), (b1, bv.at[0]), (b2, bv.at[1])))]
    for m in moves:
        m.start()
    exchange(0).greet()
    bufs[5][...] = jnp.zeros(bufs[5].shape, F32)
    bufs[3][...] = jnp.zeros(bufs[3].shape, F32)
    cells[...] = jnp.zeros(cells.shape, F32)

    def clear(f):
        xc[f, 0, 0] = jnp.zeros((64, 384), BF16)
        xc[f, 32, 1] = jnp.zeros((64, 384), BF16)

    loop(3, clear)
    for m in moves:
        m.wait()

    def first(f):
        near = img[f, :, :, 0:16].reshape(64, 16, 128).astype(F32)[:, 0]
        far = img[f, :, :, 48:64].reshape(64, 16, 128).astype(F32)[:, 15]
        edges[0, f] = near
        edges[1, f] = far
        lines[0, 3, f] = near.astype(BF16)
        lines[0, 1, f] = far.astype(BF16)
        lines[0, 0, f] = img[f, 0, 0]
        lines[0, 2, f] = img[f, 31, 1]

    loop(3, first)
    exchange(0).greeted()
    out = [pltpu.make_async_copy(img.at[f], skip.at[f], store.at[f]) for f in range(3)]

    def layer(k):
        ex = exchange(k)
        ex.start_a()
        widen(wv.at[k], wide)
        bias = jnp.concatenate([bv[k], bv[k]], axis=1)

        def prepare(f):
            img[f, 0, 0] = lines[k, 0, f]
            img[f, 31, 1] = lines[k, 2, f]
            cols[0, f] = edges[0, f]
            cols[1, f] = img[f, :, :, 0:16].reshape(64, 16, 128).astype(F32)[:, 1]
            cols[2, f] = img[f, :, :, 48:64].reshape(64, 16, 128).astype(F32)[:, 14]
            cols[3, f] = edges[1, f]
            build(f, img, xc, edges)

        loop(3, prepare)

        def face(f):
            inner(f, xc, wide, bias, img)

            @pl.when(k == 1)
            def _():
                pltpu.make_async_copy(img.at[f], skip.at[f], store.at[f]).start()

            @pl.when(f == 0)
            def _():
                ex.stage_b()

            @pl.when(f == 1)
            def _():
                ex.stage_c()
                ex.start_d()

        loop(3, face)
        ex.finish()
        loop(3, lambda f: ring(f, halo.at[k], cells.at[k], xc, cols, g, rl, wv[k].reshape(1152, 128), bv[k],
                               lines.at[k + 1], edges))
        ex.wait_sends()

    loop(2, layer)
    ring_out[...] = lines[2]
    for o in out:
        o.wait()


def main(x, nf, ori, w1, b1, w2, b2):
    vm = pl.BlockSpec(memory_space=pltpu.VMEM)
    hbm = pl.BlockSpec(memory_space=pl.ANY)
    V = pltpu.VMEM
    return pl.pallas_call(
        main_kernel,
        in_specs=[hbm] * 7,
        out_specs=[hbm, vm],
        out_shape=[jax.ShapeDtypeStruct((3, 32, 2, 64, 128), BF16), jax.ShapeDtypeStruct((4, 3, 64, 128), BF16)],
        scratch_shapes=[
            V((3, 32, 2, 64, 128), BF16),
            pltpu.SMEM((8, 12), jnp.int32), pltpu.SMEM((8, 12), jnp.int32),
            V((3, 33, 2, 64, 384), BF16),
            V((2, 3, 3, 128, 128), BF16), V((2, 1, 128), F32),
            V((1536, 256), BF16),
            V((3, 4, 3, 64, 128), BF16), V((2, 4, 3, 64, 128), BF16),
            V((2, 4, 8, 128), F32),
            V((4, 3, 64, 128), F32), V((2, 3, 64, 128), F32),
            V((2, 72, 384), F32), V((256, 1152), BF16),
            pltpu.SemaphoreType.DMA((7,)), pltpu.SemaphoreType.DMA((3,)),
        ] + EXCHANGE_SCRATCH,
        compiler_params=pltpu.CompilerParams(collective_id=0, has_side_effects=True, vmem_limit_bytes=58 * 2**20),
    )(x.reshape(3, 32, 2, 64, 128), nf.T, ori.T, w1, b1.reshape(1, 128), w2, b2.reshape(1, 128))


def last_kernel(s, rim, wd_ref, bd_ref, out, coarse, wd, g32):
    f, g = pl.program_id(0), pl.program_id(1)
    P = s.shape[1]

    @pl.when(jnp.logical_and(f == 0, g == 0))
    def _():
        build_wd(wd_ref, wd)

    col = lax.broadcasted_iota(jnp.int32, (2 * P, 8, 128), 1)
    rows = pl.ds(pl.multiple_of(2 * P * g, 16), 2 * P)
    v = s[0].reshape(2 * P, 64, 128)
    wide = v.astype(F32)
    first = jnp.where(col == 0, rim[3, f, rows].astype(F32)[:, None, :], wide[:, 0:8])
    last = jnp.where(col == 7, rim[1, f, rows].astype(F32)[:, None, :], wide[:, 56:64])
    wide = jnp.concatenate([first, wide[:, 8:56], last], axis=1).reshape(P, 2, 64, 128)
    for a in range(2):
        g32[a] = wide[:, a].reshape(P * 64, 128)

    @pl.when(g == 0)
    def _():
        g32[0, 0:64] = rim[0, f].astype(F32)

    @pl.when(g == pl.num_programs(1) - 1)
    def _():
        g32[1, pl.ds((P - 1) * 64, 64)] = rim[2, f].astype(F32)

    for a in range(2):
        out[0, :, a] = g32[a].astype(BF16).reshape(P, 64, 128)
    parts = [g32[a, pl.ds(d, P * 32, stride=2), :] for d in range(2) for a in range(2)]
    q = jnp.concatenate(parts, axis=1).astype(BF16)
    cc = jnp.dot(q, wd[...], preferred_element_type=F32) + bd_ref[...]
    coarse[0] = cc.astype(BF16).reshape(P, 32, 256)


def last(s, rim, wd, bd, P=32):
    full = lambda *shape: pl.BlockSpec(shape, lambda f, g: (0,) * len(shape))
    block = pl.BlockSpec((1, P, 2, 64, 128), lambda f, g: (f, g, 0, 0, 0))
    skip, coarse = pl.pallas_call(
        last_kernel, grid=(3, 32 // P),
        in_specs=[block, full(4, 3, 64, 128), full(2, 2, 128, 256), full(1, 256)],
        out_specs=[block, pl.BlockSpec((1, P, 32, 256), lambda f, g: (f, g, 0, 0))],
        out_shape=[jax.ShapeDtypeStruct((3, 32, 2, 64, 128), BF16), jax.ShapeDtypeStruct((3, 32, 32, 256), BF16)],
        scratch_shapes=[pltpu.VMEM((512, 256), BF16), pltpu.VMEM((2, P * 64, 128), F32)],
        compiler_params=pltpu.CompilerParams(vmem_limit_bytes=58 * 2**20, dimension_semantics=("arbitrary", "arbitrary")),
    )(s, rim, wd, bd.reshape(1, 256))
    return skip.reshape(3, 64, 64, 128), coarse


def per_device(field, conv1_w, conv1_b, conv2_w, conv2_b, down_w, down_b, neighbour_face, orientation):
    s, rim = main(field, neighbour_face, orientation, conv1_w, conv1_b, conv2_w, conv2_b)
    return last(s, rim, down_w, down_b)


def solution(mesh):
    return jax.shard_map(
        per_device, mesh=mesh,
        in_specs=(P("face", "row", "col", None), P(), P(), P(), P(), P(), P(), P(), P()),
        out_specs=(P("face", "row", "col", None), P("face", "row", "col", None)),
        check_vma=False,
    )
```

```python
import jax
import jax.numpy as jnp
from jax import lax
from jax.experimental import pallas as pl
from jax.experimental.pallas import tpu as pltpu
from jax.sharding import PartitionSpec as P

MESH = pl.DeviceIdType.MESH
F32, BF16 = jnp.float32, jnp.bfloat16
PAIRS = 16

COEF = (0.7978842854499817, 0.03633414953947067, -3.302673940197565e-05, -5.5273376347031444e-05, 3.974068931711372e-06, -1.3378310370626423e-07, 1.8139250101967264e-09)

def gelu(v):
    s = jnp.minimum(v * v, 64.0)
    p = COEF[-1] * s + COEF[-2]
    for k in COEF[-3::-1]:
        p = p * s + k
    h = 0.5 * v
    return h + h * jnp.tanh(p * v)

def build_wd(wd_ref, wd):
    for d in range(2):
        for a in range(2):
            wd[pl.ds((d*2+a)*128, 128), :] = wd_ref[a, d]

def loop(count, body):
    def step(k, _):
        body(k)
        return 0

    lax.fori_loop(0, count, step, 0)


class Exchange:
    def __init__(self, lines, halo, cells, nf, ori, pool, send_b, recv_b, tip_s, tip_r, end_s, end_r, sems, seen):
        self.lines, self.halo, self.cells, self.nf, self.ori = lines, halo, cells, nf, ori
        self.pool, self.send_b, self.recv_b = pool, send_b, recv_b
        self.tip_s, self.tip_r, self.end_s, self.end_r = tip_s, tip_r, end_s, end_r
        (self.hs, self.hr, self.as_, self.ar, self.bs, self.br, self.ts, self.tr, self.es, self.er) = sems
        self.pool_w, self.recv_w, self.tip_w = seen
        self.face, self.row, self.col = lax.axis_index("face"), lax.axis_index("row"), lax.axis_index("col")
        self.top, self.bottom = self.row == 0, self.row == 7
        self.left, self.right = self.col == 0, self.col == 7
        self.has_h = jnp.logical_or(self.top, self.bottom)
        self.has_v = jnp.logical_or(self.left, self.right)
        self.corner = jnp.logical_and(self.has_h, self.has_v)
        self.rim = jnp.logical_or(self.has_h, self.has_v)
        self.edge_h = jnp.where(self.top, 0, 2)
        self.edge_v = jnp.where(self.left, 3, 1)
        self.tip = jnp.where(self.top, jnp.where(self.left, 0, 1), jnp.where(self.left, 3, 2))

    def own(self, which):
        flat = which == 0
        has = jnp.logical_or(jnp.logical_and(flat, self.has_h), jnp.logical_and(jnp.logical_not(flat), self.has_v))
        edge = jnp.where(flat, self.edge_h, self.edge_v)
        seg = jnp.where(flat, self.col, self.row)
        return has, edge, seg, edge * 2 + jnp.where(seg >= 4, 1, 0)

    def beside(self, side):
        r = self.row + jnp.where(side == 0, -1, jnp.where(side == 2, 1, 0))
        c = self.col + jnp.where(side == 1, 1, jnp.where(side == 3, -1, 0))
        ok = jnp.logical_and(jnp.logical_and(r >= 0, r <= 7), jnp.logical_and(c >= 0, c <= 7))
        return ok, (self.face, r, c)

    def classmate(self, k):
        which, q = lax.div(k, 8), lax.rem(k, 8)
        has, edge, seg, slot = self.own(which)
        low = jnp.where(seg >= 4, 7 - seg, seg)
        s = jnp.where(lax.rem(q, 2) == 0, low, 7 - low)
        e = lax.div(q, 2)
        r = jnp.where(e == 0, 0, jnp.where(e == 2, 7, s))
        c = jnp.where(e == 1, 7, jnp.where(e == 3, 0, s))
        other = jnp.logical_or(r != self.row, c != self.col)
        once = jnp.logical_or(low > 0, lax.rem(q, 4) < 2)
        return which, q, edge, slot, jnp.logical_and(has, jnp.logical_and(other, once)), (self.face, r, c)

    def across(self, d):
        return (lax.rem(self.face + d, 4), self.row, self.col)

    def greet(self):
        barrier = pltpu.get_barrier_semaphore()

        def meet(ok, dev):
            @pl.when(ok)
            def _():
                pl.semaphore_signal(barrier, inc=1, device_id=dev, device_id_type=MESH)

        loop(4, lambda k: meet(*self.beside(k)))
        loop(16, lambda k: meet(*self.classmate(k)[4:]))
        loop(3, lambda k: meet(self.rim, self.across(k + 1)))

    def greeted(self):
        barrier = pltpu.get_barrier_semaphore()

        near = sum(jnp.where(end, 0, 1) for end in (self.top, self.bottom, self.left, self.right))
        far = jnp.where(self.corner, 9, jnp.where(self.rim, 10, 0))
        pl.semaphore_wait(barrier, near + far)

    def copy_beside(self, side):
        ok, dev = self.beside(side)
        there = lax.rem(side + 2, 4)
        return ok, pltpu.make_async_remote_copy(
            self.lines.at[side], self.halo.at[there], self.hs.at[side], self.hr.at[there],
            device_id=dev, device_id_type=MESH)

    def copy_class(self, k):
        which, q, edge, slot, ok, dev = self.classmate(k)
        return ok, pltpu.make_async_remote_copy(
            self.lines.at[edge], self.pool.at[slot], self.as_.at[which, q], self.ar.at[slot],
            device_id=dev, device_id_type=MESH)

    def copy_across(self, k):
        which, d = lax.div(k, 3), lax.rem(k, 3) + 1
        return self.own(which)[0], pltpu.make_async_remote_copy(
            self.send_b.at[which, d], self.recv_b.at[which, self.face], self.bs.at[which, d],
            self.br.at[which, self.face], device_id=self.across(d), device_id_type=MESH)

    def copy_tip(self, k):
        d = k + 1
        return self.corner, pltpu.make_async_remote_copy(
            self.tip_s.at[d], self.tip_r.at[self.face], self.ts.at[d], self.tr.at[self.face],
            device_id=self.across(d), device_id_type=MESH)

    def copy_end(self, side):
        ok, dev = self.beside(side)
        there = lax.rem(side + 2, 4)
        ok = jnp.logical_and(ok, jnp.logical_or(lax.rem(side, 2) == 1, self.has_v))
        return ok, pltpu.make_async_remote_copy(
            self.end_s.at[side], self.end_r.at[there], self.es.at[side], self.er.at[there],
            device_id=dev, device_id_type=MESH)

    @staticmethod
    def start(pair):
        ok, copy = pair

        @pl.when(ok)
        def _():
            copy.start()

    @staticmethod
    def sent(pair):
        ok, copy = pair

        @pl.when(ok)
        def _():
            copy.wait_send()

    @staticmethod
    def landed(ok, dst, sem):
        @pl.when(ok)
        def _():
            pltpu.make_async_copy(dst, dst, sem).wait()

    def start_a(self):
        loop(16, lambda k: self.start(self.copy_class(k)))
        loop(4, lambda k: self.start(self.copy_beside(k)))

        def keep(which):
            has, edge, seg, slot = self.own(which)

            @pl.when(has)
            def _():
                self.pool[slot] = self.lines[edge]

        loop(2, keep)

    def picked(self, which, face, i):
        has, edge, seg, slot = self.own(which)
        n, o = self.nf[edge, face * 3 + i], self.ori[edge, face * 3 + i]
        side, turned = lax.div(o, 2), lax.rem(o, 2)
        s = jnp.where(turned == 1, 7 - seg, seg)
        return self.pool_w[side * 2 + jnp.where(s >= 4, 1, 0), lax.rem(n, 3)]

    def picked_tip(self, face, i):
        n, k = jnp.minimum(self.nf[4 + self.tip, face * 3 + i], 11), self.ori[4 + self.tip, face * 3 + i]
        line = self.pool_w[jnp.where(k == 2, 5, jnp.where(k == 3, 4, k)), lax.rem(n, 3)].astype(F32)
        return jnp.where(jnp.logical_or(k == 1, k == 2), line[63:64], line[0:1])

    def stage_b(self):
        @pl.when(self.rim)
        def _():
            slot_h, slot_v = self.own(0)[3], self.own(1)[3]

            def arrived(q):
                mine = jnp.logical_or(
                    jnp.logical_and(self.has_h, slot_h == q), jnp.logical_and(self.has_v, slot_v == q))
                self.landed(jnp.logical_not(mine), self.pool.at[q], self.ar.at[q])

            loop(8, arrived)

            def take(q):
                self.pool_w[q] = self.pool[q]

            loop(8, take)

            def pick(k):
                at = lax.rem(k, 4)
                which, d = lax.div(k, 4), jnp.where(at == 0, 2, jnp.where(at == 1, 1, jnp.where(at == 2, 3, 0)))

                @pl.when(self.own(which)[0])
                def _():
                    for i in range(3):
                        self.send_b[which, d, i] = self.picked(which, self.across(d)[0], i)

                    @pl.when(d > 0)
                    def _():
                        self.copy_across(which * 3 + jnp.maximum(d - 1, 0))[1].start()

            loop(8, pick)

            @pl.when(self.corner)
            def _():
                def tips(k):
                    d = lax.rem(k + 1, 4)
                    for i in range(3):
                        self.tip_s[d, pl.ds(i, 1)] = self.picked_tip(self.across(d)[0], i)

                    @pl.when(d > 0)
                    def _():
                        self.copy_tip(jnp.maximum(d - 1, 0))[1].start()

                loop(4, tips)

    def stage_c(self):
        def arrived(k):
            which, other = lax.div(k, 3), lax.rem(self.face + 1 + lax.rem(k, 3), 4)
            self.landed(self.own(which)[0], self.recv_b.at[which, other], self.br.at[which, other])

        loop(6, arrived)

        def take(k):
            which, group = lax.div(k, 4), lax.rem(k, 4)
            has = self.own(which)[0]

            @pl.when(jnp.logical_and(has, group != self.face))
            def _():
                self.recv_w[which, group] = self.recv_b[which, group]

        loop(8, take)
        i0 = lax.broadcasted_iota(jnp.int32, (64, 64), 0)
        i1 = lax.broadcasted_iota(jnp.int32, (64, 64), 1)

        def turn(k):
            which, i = lax.div(k, 3), lax.rem(k, 3)
            has, edge, seg, slot = self.own(which)

            @pl.when(has)
            def _():
                n, o = self.nf[edge, self.face * 3 + i], self.ori[edge, self.face * 3 + i]
                group = lax.div(n, 3)
                order = jnp.where(i1 == jnp.where(lax.rem(o, 2) == 1, 63 - i0, i0), 1.0, 0.0).astype(BF16)
                line = jnp.where(group == self.face, self.send_b[which, 0, i], self.recv_w[which, group, i])
                self.halo[edge, i] = jnp.dot(order, line, preferred_element_type=F32).astype(BF16)

        loop(6, turn)
        loop(4, lambda k: self.landed(self.beside(k)[0], self.halo.at[k], self.hr.at[k]))

    def start_d(self):
        def ends(side):
            last = jnp.logical_or(side == 1, side == 2)
            for i in range(3):
                for part, line in ((0, jnp.where(lax.rem(side, 2) == 1, 0, self.edge_v)), (8, 2)):
                    v = self.halo[line, i].astype(F32)
                    self.end_s[side, pl.ds(part + i, 1)] = jnp.where(last, v[63:64], v[0:1])

            self.start(self.copy_end(side))

        loop(4, ends)

    def finish(self):
        loop(4, lambda k: self.landed(self.copy_end_ok(k), self.end_r.at[k], self.er.at[k]))

        @pl.when(self.corner)
        def _():
            def arrived(k):
                other = lax.rem(self.face + 1 + k, 4)
                self.landed(self.corner, self.tip_r.at[other], self.tr.at[other])

            loop(3, arrived)
            self.tip_w[...] = self.tip_r[...]
            for i in range(3):
                n = self.nf[4 + self.tip, self.face * 3 + i]
                group = lax.div(jnp.minimum(n, 11), 3)
                got = jnp.where(group == self.face, self.tip_s[0, pl.ds(i, 1)], self.tip_w[group, pl.ds(i, 1)])
                self.cells[self.tip, pl.ds(i, 1)] = jnp.where(n < 12, got, 0.0)

        not_, and_ = jnp.logical_not, jnp.logical_and
        for cell, flat, part, flat_side, upright, up_side in (
            (0, not_(self.left), 0, 3, not_(self.top), 0),
            (1, not_(self.right), 0, 1, not_(self.top), 0),
            (2, not_(self.right), 8, 1, not_(self.bottom), 2),
            (3, not_(self.left), 8, 3, not_(self.bottom), 2),
        ):
            @pl.when(flat)
            def _(cell=cell, part=part, flat_side=flat_side):
                self.cells[cell] = self.end_r[flat_side, pl.ds(part, 8)]

            @pl.when(and_(not_(flat), upright))
            def _(cell=cell, up_side=up_side):
                self.cells[cell] = self.end_r[up_side, pl.ds(0, 8)]

    def copy_end_ok(self, side):
        ok, dev = self.beside(side)
        return jnp.logical_and(ok, jnp.logical_or(lax.rem(side, 2) == 1, self.has_v))

    def wait_sends(self):
        loop(4, lambda k: self.sent(self.copy_beside(k)))
        loop(16, lambda k: self.sent(self.copy_class(k)))
        loop(6, lambda k: self.sent(self.copy_across(k)))
        loop(3, lambda k: self.sent(self.copy_tip(k)))
        loop(4, lambda k: self.sent(self.copy_end(k)))


EXCHANGE_SCRATCH = [
    pltpu.VMEM((2, 8, 3, 64, 128), BF16),
    pltpu.VMEM((2, 2, 4, 3, 64, 128), BF16),
    pltpu.VMEM((2, 2, 4, 3, 64, 128), BF16),
    pltpu.VMEM((2, 4, 8, 128), F32),
    pltpu.VMEM((2, 4, 8, 128), F32),
    pltpu.VMEM((2, 4, 16, 128), F32),
    pltpu.VMEM((2, 4, 16, 128), F32),
    pltpu.VMEM((8, 3, 64, 128), BF16), pltpu.VMEM((2, 4, 3, 64, 128), BF16), pltpu.VMEM((4, 8, 128), F32),
    pltpu.SemaphoreType.DMA((2, 4)), pltpu.SemaphoreType.DMA((2, 4)),
    pltpu.SemaphoreType.DMA((2, 2, 8)), pltpu.SemaphoreType.DMA((2, 8)),
    pltpu.SemaphoreType.DMA((2, 2, 4)), pltpu.SemaphoreType.DMA((2, 2, 4)),
    pltpu.SemaphoreType.DMA((2, 4)), pltpu.SemaphoreType.DMA((2, 4)),
    pltpu.SemaphoreType.DMA((2, 4)), pltpu.SemaphoreType.DMA((2, 4)),
]


def widen(w, out):
    out[...] = jnp.zeros(out.shape, BF16)
    for d in range(3):
        for p in range(2):
            for a in range(3):
                out[pl.ds((a + p) * 384 + d * 128, 128), pl.ds(p * 128, 128)] = w[a, d]


def build(f, img, xc, edges):
    col = lax.broadcasted_iota(jnp.int32, (8, 8, 128), 1)

    def rows(g):
        v = img[f, pl.ds(4 * g, 4)].reshape(8, 64, 128)
        wide = v.astype(F32)
        at = pl.ds(pl.multiple_of(8 * g, 8), 8)
        first = jnp.where(col == 0, edges[0, f, at][:, None, :], wide[:, 0:8])
        last = jnp.where(col == 7, edges[1, f, at][:, None, :], wide[:, 56:64])
        wide = jnp.concatenate([first, wide[:, 8:56], last], axis=1)
        parts = [pltpu.roll(wide, 1, 1).astype(BF16), wide.astype(BF16), pltpu.roll(wide, 63, 1).astype(BF16)]
        for i in range(8):
            k = 1 + i
            for d in range(3):
                xc[f, 4 * g + k // 2, k % 2, :, d * 128:(d + 1) * 128] = parts[d][i]

    loop(8, rows)


def inner(f, xc, w2, bias, img):
    def chunk(g):
        lhs = jnp.concatenate(
            [xc[f, pl.ds(PAIRS * g + t // 2, PAIRS), t % 2].reshape(PAIRS * 64, 384) for t in range(4)], axis=1)
        o = gelu(jnp.dot(lhs, w2[...], preferred_element_type=F32) + bias).astype(BF16)
        for p in range(2):
            img[f, pl.ds(PAIRS * g, PAIRS), p] = o[:, p * 128:(p + 1) * 128].reshape(PAIRS, 64, 128)

    loop(32 // PAIRS, chunk)


SIDES = ((0, 3, 0, 128, 0), (1, 1, 256, 0, 62))


def ring_ready(f, xc, cols, g, rl, fix):
    for e, r, x0 in ((0, ((0, 1), (1, 0)), 384), (2, ((31, 1), (32, 0)), 0)):
        for k in range(2):
            rl[f, pl.ds(e * 64, 64), pl.ds(x0 + k * 384, 384)] = xc[f, r[k][0], r[k][1]]
    for side, e, rim, own, px in SIDES:
        for k in range(2):
            g[side, pl.ds(1, 64), pl.ds(k * 128, 128)] = cols[2 * side + k, f]
        for a in range(3):
            to = pl.ds(a * 384 + own, 256)
            rl[f, pl.ds(e * 64, 64), to] = g[side, pl.ds(a, 64)].astype(BF16)
            for tip, at in (((0, 1)[side], 0), ((3, 2)[side], 63)):
                fix[f, tip:tip + 1, to] = g[side, a + at:a + at + 1]


def ring(f, halo, rl, fix, w, bias, out):
    for e in range(4):
        mid = halo[e, f]
        wide = mid.astype(F32)
        parts = (pltpu.roll(wide, 1, 0).astype(BF16), mid, pltpu.roll(wide, 63, 0).astype(BF16))
        lane, step = ((0, 128), (256, 384), (768, 128), (0, 384))[e]
        for k in range(3):
            rl[f, pl.ds(e * 64, 64), pl.ds(lane + k * step, 128)] = parts[k]
        if e % 2 == 0:
            a = e * 384
            for side, _, rim, own, px in SIDES:
                tip = ((0, 1), (3, 2))[e // 2][side]
                for k in range(2):
                    fix[f, tip:tip + 1, pl.ds(a + own + k * 128, 128)] = wide[px + k:px + k + 1]
        else:
            for tip, a, at in (((1, 0)[e // 2], 384, 0), ((2, 3)[e // 2], 0, 62)):
                for k in range(2):
                    fix[f, tip:tip + 1, pl.ds(a + lane + k * 384, 128)] = wide[at + k:at + k + 1]
    out[f] = gelu(jnp.dot(rl[f], w, preferred_element_type=F32) + bias)


def corners(cells, fix, w, bias, out):
    for f in range(3):
        for tip, lane in ((0, 0), (1, 256), (2, 768 + 256), (3, 768)):
            fix[f, tip:tip + 1, pl.ds(lane, 128)] = cells[tip, f:f + 1]
    o = gelu(jnp.dot(fix[...].reshape(24, 1152).astype(BF16), w, preferred_element_type=F32) + bias)
    for f in range(3):
        for tip, at in ((0, 192), (1, 64), (2, 127), (3, 255)):
            out[f, at:at + 1] = o[8 * f + tip:8 * f + tip + 1]


def settle(f, o, out, edges):
    row = lax.broadcasted_iota(jnp.int32, (64, 128), 0)
    left, right = o[f, 192:256], o[f, 64:128]
    out[3, f] = left.astype(BF16)
    out[1, f] = right.astype(BF16)
    edges[0, f] = left
    edges[1, f] = right
    for e, k in ((0, 0), (2, 63)):
        line = jnp.where(row == 0, left[k:k + 1], jnp.where(row == 63, right[k:k + 1], o[f, e * 64:(e + 1) * 64]))
        out[e, f] = line.astype(BF16)


def main_kernel(x, nf_in, ori_in, w1, b1, w2, b2, skip, ring_out,
                img, nf, ori, xc, wv, bv, wide, lines, halo, cells, cols, edges, g, rl, fix, rims, load, store, *rest):
    bufs, seen, sems = rest[:7], rest[7:10], rest[10:]

    def exchange(layer):
        return Exchange(lines.at[layer], halo.at[layer], cells.at[layer], nf, ori,
                        *[b.at[layer] for b in bufs], [s.at[layer] for s in sems], seen)

    ends, middle = (pl.ds(0, 16), pl.ds(48, 16)), pl.ds(16, 32)
    moves = [pltpu.make_async_copy(src, dst, load.at[k]) for k, (src, dst) in enumerate((
        (x.at[:, :, :, ends[0]], img.at[:, :, :, ends[0]]), (x.at[:, :, :, ends[1]], img.at[:, :, :, ends[1]]),
        (x.at[:, 0, 0], lines.at[0, 0]), (x.at[:, 31, 1], lines.at[0, 2]),
        (x.at[:, :, :, middle], img.at[:, :, :, middle]),
        (w1, wv.at[0]), (b1, bv.at[0]), (nf_in, nf), (ori_in, ori), (w2, wv.at[1]), (b2, bv.at[1])))]
    for m in moves:
        m.start()
    exchange(0).greet()
    bufs[5][...] = jnp.zeros(bufs[5].shape, F32)
    bufs[3][...] = jnp.zeros(bufs[3].shape, F32)
    cells[...] = jnp.zeros(cells.shape, F32)
    fix[...] = jnp.zeros(fix.shape, F32)
    g[...] = jnp.zeros(g.shape, F32)

    def clear(f):
        xc[f, 0, 0] = jnp.zeros((64, 384), BF16)
        xc[f, 32, 1] = jnp.zeros((64, 384), BF16)

    loop(3, clear)
    for m in moves[:4]:
        m.wait()

    def first(f):
        near = img[f, :, :, 0:16].reshape(64, 16, 128).astype(F32)[:, 0]
        far = img[f, :, :, 48:64].reshape(64, 16, 128).astype(F32)[:, 15]
        edges[0, f] = near
        edges[1, f] = far
        lines[0, 3, f] = near.astype(BF16)
        lines[0, 1, f] = far.astype(BF16)

    loop(3, first)
    exchange(0).greeted()
    out = [pltpu.make_async_copy(img.at[f], skip.at[f], store.at[f]) for f in range(3)]

    def layer(k):
        ex = exchange(k)
        ex.start_a()

        @pl.when(k == 0)
        def _():
            for m in moves[4:]:
                m.wait()

        widen(wv.at[k], wide)
        bias = jnp.concatenate([bv[k], bv[k]], axis=1)

        def prepare(f):
            img[f, 0, 0] = lines[k, 0, f]
            img[f, 31, 1] = lines[k, 2, f]
            cols[0, f] = edges[0, f]
            cols[1, f] = img[f, :, :, 0:16].reshape(64, 16, 128).astype(F32)[:, 1]
            cols[2, f] = img[f, :, :, 48:64].reshape(64, 16, 128).astype(F32)[:, 14]
            cols[3, f] = edges[1, f]

        loop(3, prepare)

        def face(f):
            build(f, img, xc, edges)
            inner(f, xc, wide, bias, img)

            @pl.when(k == 1)
            def _():
                pltpu.make_async_copy(img.at[f], skip.at[f], store.at[f]).start()

            @pl.when(f == 0)
            def _():
                ex.stage_b()

        loop(3, face)
        loop(3, lambda f: ring_ready(f, xc, cols, g, rl, fix))
        ex.stage_c()
        ex.start_d()
        w = wv[k].reshape(1152, 128)
        loop(3, lambda f: ring(f, halo.at[k], rl, fix, w, bv[k], rims))
        ex.finish()
        corners(cells.at[k], fix, w, bv[k], rims)
        loop(3, lambda f: settle(f, rims, lines.at[k + 1], edges))
        ex.wait_sends()

    loop(2, layer)
    ring_out[...] = lines[2]
    for o in out:
        o.wait()


def main(x, nf, ori, w1, b1, w2, b2):
    vm = pl.BlockSpec(memory_space=pltpu.VMEM)
    hbm = pl.BlockSpec(memory_space=pl.ANY)
    V = pltpu.VMEM
    return pl.pallas_call(
        main_kernel,
        in_specs=[hbm] * 7,
        out_specs=[hbm, vm],
        out_shape=[jax.ShapeDtypeStruct((3, 32, 2, 64, 128), BF16), jax.ShapeDtypeStruct((4, 3, 64, 128), BF16)],
        scratch_shapes=[
            V((3, 32, 2, 64, 128), BF16),
            pltpu.SMEM((8, 12), jnp.int32), pltpu.SMEM((8, 12), jnp.int32),
            V((3, 33, 2, 64, 384), BF16),
            V((2, 3, 3, 128, 128), BF16), V((2, 1, 128), F32),
            V((1536, 256), BF16),
            V((3, 4, 3, 64, 128), BF16), V((2, 4, 3, 64, 128), BF16),
            V((2, 4, 8, 128), F32),
            V((4, 3, 64, 128), F32), V((2, 3, 64, 128), F32),
            V((2, 72, 256), F32), V((3, 256, 1152), BF16),
            V((3, 8, 1152), F32), V((3, 256, 128), F32),
            pltpu.SemaphoreType.DMA((11,)), pltpu.SemaphoreType.DMA((3,)),
        ] + EXCHANGE_SCRATCH,
        compiler_params=pltpu.CompilerParams(collective_id=0, has_side_effects=True, vmem_limit_bytes=58 * 2**20),
    )(x.reshape(3, 32, 2, 64, 128), nf.T, ori.T, w1, b1.reshape(1, 128), w2, b2.reshape(1, 128))


def last_kernel(s, rim, wd_ref, bd_ref, out, coarse, wd, g32):
    f, g = pl.program_id(0), pl.program_id(1)
    P = s.shape[1]

    @pl.when(jnp.logical_and(f == 0, g == 0))
    def _():
        build_wd(wd_ref, wd)

    col = lax.broadcasted_iota(jnp.int32, (2 * P, 8, 128), 1)
    rows = pl.ds(pl.multiple_of(2 * P * g, 16), 2 * P)
    v = s[0].reshape(2 * P, 64, 128)
    wide = v.astype(F32)
    first = jnp.where(col == 0, rim[3, f, rows].astype(F32)[:, None, :], wide[:, 0:8])
    last = jnp.where(col == 7, rim[1, f, rows].astype(F32)[:, None, :], wide[:, 56:64])
    wide = jnp.concatenate([first, wide[:, 8:56], last], axis=1).reshape(P, 2, 64, 128)
    for a in range(2):
        g32[a] = wide[:, a].reshape(P * 64, 128)

    @pl.when(g == 0)
    def _():
        g32[0, 0:64] = rim[0, f].astype(F32)

    @pl.when(g == pl.num_programs(1) - 1)
    def _():
        g32[1, pl.ds((P - 1) * 64, 64)] = rim[2, f].astype(F32)

    for a in range(2):
        out[0, :, a] = g32[a].astype(BF16).reshape(P, 64, 128)
    parts = [g32[a, pl.ds(d, P * 32, stride=2), :] for d in range(2) for a in range(2)]
    q = jnp.concatenate(parts, axis=1).astype(BF16)
    cc = jnp.dot(q, wd[...], preferred_element_type=F32) + bd_ref[...]
    coarse[0] = cc.astype(BF16).reshape(P, 32, 256)


def last(s, rim, wd, bd, P=32):
    full = lambda *shape: pl.BlockSpec(shape, lambda f, g: (0,) * len(shape))
    block = pl.BlockSpec((1, P, 2, 64, 128), lambda f, g: (f, g, 0, 0, 0))
    skip, coarse = pl.pallas_call(
        last_kernel, grid=(3, 32 // P),
        in_specs=[block, full(4, 3, 64, 128), full(2, 2, 128, 256), full(1, 256)],
        out_specs=[block, pl.BlockSpec((1, P, 32, 256), lambda f, g: (f, g, 0, 0))],
        out_shape=[jax.ShapeDtypeStruct((3, 32, 2, 64, 128), BF16), jax.ShapeDtypeStruct((3, 32, 32, 256), BF16)],
        scratch_shapes=[pltpu.VMEM((512, 256), BF16), pltpu.VMEM((2, P * 64, 128), F32)],
        compiler_params=pltpu.CompilerParams(vmem_limit_bytes=58 * 2**20, dimension_semantics=("arbitrary", "arbitrary")),
    )(s, rim, wd, bd.reshape(1, 256))
    return skip.reshape(3, 64, 64, 128), coarse


def per_device(field, conv1_w, conv1_b, conv2_w, conv2_b, down_w, down_b, neighbour_face, orientation):
    s, rim = main(field, neighbour_face, orientation, conv1_w, conv1_b, conv2_w, conv2_b)
    return last(s, rim, down_w, down_b)


def solution(mesh):
    return jax.shard_map(
        per_device, mesh=mesh,
        in_specs=(P("face", "row", "col", None), P(), P(), P(), P(), P(), P(), P(), P()),
        out_specs=(P("face", "row", "col", None), P("face", "row", "col", None)),
        check_vma=False,
    )
```

```python
import jax
import jax.numpy as jnp
from jax import lax
from jax.experimental import pallas as pl
from jax.experimental.pallas import tpu as pltpu
from jax.sharding import PartitionSpec as P

MESH = pl.DeviceIdType.MESH
F32, BF16 = jnp.float32, jnp.bfloat16
PAIRS = 16

COEF = (0.7978842854499817, 0.03633414953947067, -3.302673940197565e-05, -5.5273376347031444e-05, 3.974068931711372e-06, -1.3378310370626423e-07, 1.8139250101967264e-09)

def gelu(v):
    s = jnp.minimum(v * v, 64.0)
    p = COEF[-1] * s + COEF[-2]
    for k in COEF[-3::-1]:
        p = p * s + k
    h = 0.5 * v
    return h + h * jnp.tanh(p * v)

def build_wd(wd_ref, wd):
    for d in range(2):
        for a in range(2):
            wd[pl.ds((d*2+a)*128, 128), :] = wd_ref[a, d]

def loop(count, body):
    def step(k, _):
        body(k)
        return 0

    lax.fori_loop(0, count, step, 0)


class Exchange:
    def __init__(self, lines, halo, cells, nf, ori, pool, send_b, recv_b, tip_s, tip_r, end_s, end_r, sems, seen):
        self.lines, self.halo, self.cells, self.nf, self.ori = lines, halo, cells, nf, ori
        self.pool, self.send_b, self.recv_b = pool, send_b, recv_b
        self.tip_s, self.tip_r, self.end_s, self.end_r = tip_s, tip_r, end_s, end_r
        (self.hs, self.hr, self.as_, self.ar, self.bs, self.br, self.ts, self.tr, self.es, self.er) = sems
        self.pool_w, self.recv_w, self.tip_w = seen
        self.face, self.row, self.col = lax.axis_index("face"), lax.axis_index("row"), lax.axis_index("col")
        self.top, self.bottom = self.row == 0, self.row == 7
        self.left, self.right = self.col == 0, self.col == 7
        self.has_h = jnp.logical_or(self.top, self.bottom)
        self.has_v = jnp.logical_or(self.left, self.right)
        self.corner = jnp.logical_and(self.has_h, self.has_v)
        self.rim = jnp.logical_or(self.has_h, self.has_v)
        self.edge_h = jnp.where(self.top, 0, 2)
        self.edge_v = jnp.where(self.left, 3, 1)
        self.tip = jnp.where(self.top, jnp.where(self.left, 0, 1), jnp.where(self.left, 3, 2))

    def own(self, which):
        flat = which == 0
        has = jnp.logical_or(jnp.logical_and(flat, self.has_h), jnp.logical_and(jnp.logical_not(flat), self.has_v))
        edge = jnp.where(flat, self.edge_h, self.edge_v)
        seg = jnp.where(flat, self.col, self.row)
        return has, edge, seg, edge * 2 + jnp.where(seg >= 4, 1, 0)

    def beside(self, side):
        r = self.row + jnp.where(side == 0, -1, jnp.where(side == 2, 1, 0))
        c = self.col + jnp.where(side == 1, 1, jnp.where(side == 3, -1, 0))
        ok = jnp.logical_and(jnp.logical_and(r >= 0, r <= 7), jnp.logical_and(c >= 0, c <= 7))
        return ok, (self.face, r, c)

    def classmate(self, k):
        which, q = lax.div(k, 8), lax.rem(k, 8)
        has, edge, seg, slot = self.own(which)
        low = jnp.where(seg >= 4, 7 - seg, seg)
        s = jnp.where(lax.rem(q, 2) == 0, low, 7 - low)
        e = lax.div(q, 2)
        r = jnp.where(e == 0, 0, jnp.where(e == 2, 7, s))
        c = jnp.where(e == 1, 7, jnp.where(e == 3, 0, s))
        other = jnp.logical_or(r != self.row, c != self.col)
        once = jnp.logical_or(low > 0, lax.rem(q, 4) < 2)
        return which, q, edge, slot, jnp.logical_and(has, jnp.logical_and(other, once)), (self.face, r, c)

    def across(self, d):
        return (lax.rem(self.face + d, 4), self.row, self.col)

    def greet(self):
        barrier = pltpu.get_barrier_semaphore()

        def meet(ok, dev):
            @pl.when(ok)
            def _():
                pl.semaphore_signal(barrier, inc=1, device_id=dev, device_id_type=MESH)

        loop(4, lambda k: meet(*self.beside(k)))
        loop(16, lambda k: meet(*self.classmate(k)[4:]))
        loop(3, lambda k: meet(self.rim, self.across(k + 1)))

    def greeted(self):
        barrier = pltpu.get_barrier_semaphore()

        near = sum(jnp.where(end, 0, 1) for end in (self.top, self.bottom, self.left, self.right))
        far = jnp.where(self.corner, 9, jnp.where(self.rim, 10, 0))
        pl.semaphore_wait(barrier, near + far)

    def copy_beside(self, side):
        ok, dev = self.beside(side)
        there = lax.rem(side + 2, 4)
        return ok, pltpu.make_async_remote_copy(
            self.lines.at[side], self.halo.at[there], self.hs.at[side], self.hr.at[there],
            device_id=dev, device_id_type=MESH)

    def copy_class(self, k):
        which, q, edge, slot, ok, dev = self.classmate(k)
        return ok, pltpu.make_async_remote_copy(
            self.lines.at[edge], self.pool.at[slot], self.as_.at[which, q], self.ar.at[slot],
            device_id=dev, device_id_type=MESH)

    def copy_across(self, k):
        which, d = lax.div(k, 3), lax.rem(k, 3) + 1
        return self.own(which)[0], pltpu.make_async_remote_copy(
            self.send_b.at[which, d], self.recv_b.at[which, self.face], self.bs.at[which, d],
            self.br.at[which, self.face], device_id=self.across(d), device_id_type=MESH)

    def copy_tip(self, k):
        d = k + 1
        return self.corner, pltpu.make_async_remote_copy(
            self.tip_s.at[d], self.tip_r.at[self.face], self.ts.at[d], self.tr.at[self.face],
            device_id=self.across(d), device_id_type=MESH)

    def copy_end(self, side):
        ok, dev = self.beside(side)
        there = lax.rem(side + 2, 4)
        ok = jnp.logical_and(ok, jnp.logical_or(lax.rem(side, 2) == 1, self.has_v))
        return ok, pltpu.make_async_remote_copy(
            self.end_s.at[side], self.end_r.at[there], self.es.at[side], self.er.at[there],
            device_id=dev, device_id_type=MESH)

    @staticmethod
    def start(pair):
        ok, copy = pair

        @pl.when(ok)
        def _():
            copy.start()

    @staticmethod
    def sent(pair):
        ok, copy = pair

        @pl.when(ok)
        def _():
            copy.wait_send()

    @staticmethod
    def landed(ok, dst, sem):
        @pl.when(ok)
        def _():
            pltpu.make_async_copy(dst, dst, sem).wait()

    def start_a(self):
        loop(16, lambda k: self.start(self.copy_class(k)))
        loop(4, lambda k: self.start(self.copy_beside(k)))

        def keep(which):
            has, edge, seg, slot = self.own(which)

            @pl.when(has)
            def _():
                self.pool[slot] = self.lines[edge]

        loop(2, keep)

    def picked(self, which, face, i):
        has, edge, seg, slot = self.own(which)
        n, o = self.nf[edge, face * 3 + i], self.ori[edge, face * 3 + i]
        side, turned = lax.div(o, 2), lax.rem(o, 2)
        s = jnp.where(turned == 1, 7 - seg, seg)
        return self.pool_w[side * 2 + jnp.where(s >= 4, 1, 0), lax.rem(n, 3)]

    def picked_tip(self, face, i):
        n, k = jnp.minimum(self.nf[4 + self.tip, face * 3 + i], 11), self.ori[4 + self.tip, face * 3 + i]
        line = self.pool_w[jnp.where(k == 2, 5, jnp.where(k == 3, 4, k)), lax.rem(n, 3)].astype(F32)
        return jnp.where(jnp.logical_or(k == 1, k == 2), line[63:64], line[0:1])

    def stage_b(self):
        @pl.when(self.rim)
        def _():
            slot_h, slot_v = self.own(0)[3], self.own(1)[3]

            def arrived(q):
                mine = jnp.logical_or(
                    jnp.logical_and(self.has_h, slot_h == q), jnp.logical_and(self.has_v, slot_v == q))
                self.landed(jnp.logical_not(mine), self.pool.at[q], self.ar.at[q])

            loop(8, arrived)

            def take(q):
                self.pool_w[q] = self.pool[q]

            loop(8, take)

            def pick(k):
                at = lax.rem(k, 4)
                which, d = lax.div(k, 4), jnp.where(at == 0, 2, jnp.where(at == 1, 1, jnp.where(at == 2, 3, 0)))

                @pl.when(self.own(which)[0])
                def _():
                    for i in range(3):
                        self.send_b[which, d, i] = self.picked(which, self.across(d)[0], i)

                    @pl.when(d > 0)
                    def _():
                        self.copy_across(which * 3 + jnp.maximum(d - 1, 0))[1].start()

            loop(8, pick)

            @pl.when(self.corner)
            def _():
                def tips(k):
                    d = lax.rem(k + 1, 4)
                    for i in range(3):
                        self.tip_s[d, pl.ds(i, 1)] = self.picked_tip(self.across(d)[0], i)

                    @pl.when(d > 0)
                    def _():
                        self.copy_tip(jnp.maximum(d - 1, 0))[1].start()

                loop(4, tips)

    def stage_c(self):
        def arrived(k):
            which, other = lax.div(k, 3), lax.rem(self.face + 1 + lax.rem(k, 3), 4)
            self.landed(self.own(which)[0], self.recv_b.at[which, other], self.br.at[which, other])

        loop(6, arrived)

        def take(k):
            which, group = lax.div(k, 4), lax.rem(k, 4)
            has = self.own(which)[0]

            @pl.when(jnp.logical_and(has, group != self.face))
            def _():
                self.recv_w[which, group] = self.recv_b[which, group]

        loop(8, take)
        i0 = lax.broadcasted_iota(jnp.int32, (64, 64), 0)
        i1 = lax.broadcasted_iota(jnp.int32, (64, 64), 1)

        def turn(k):
            which, i = lax.div(k, 3), lax.rem(k, 3)
            has, edge, seg, slot = self.own(which)

            @pl.when(has)
            def _():
                n, o = self.nf[edge, self.face * 3 + i], self.ori[edge, self.face * 3 + i]
                group = lax.div(n, 3)
                order = jnp.where(i1 == jnp.where(lax.rem(o, 2) == 1, 63 - i0, i0), 1.0, 0.0).astype(BF16)
                line = jnp.where(group == self.face, self.send_b[which, 0, i], self.recv_w[which, group, i])
                self.halo[edge, i] = jnp.dot(order, line, preferred_element_type=F32).astype(BF16)

        loop(6, turn)
        loop(4, lambda k: self.landed(self.beside(k)[0], self.halo.at[k], self.hr.at[k]))

    def start_d(self):
        def ends(side):
            last = jnp.logical_or(side == 1, side == 2)
            for i in range(3):
                for part, line in ((0, jnp.where(lax.rem(side, 2) == 1, 0, self.edge_v)), (8, 2)):
                    v = self.halo[line, i].astype(F32)
                    self.end_s[side, pl.ds(part + i, 1)] = jnp.where(last, v[63:64], v[0:1])

            self.start(self.copy_end(side))

        loop(4, ends)

    def finish(self):
        loop(4, lambda k: self.landed(self.copy_end_ok(k), self.end_r.at[k], self.er.at[k]))

        @pl.when(self.corner)
        def _():
            def arrived(k):
                other = lax.rem(self.face + 1 + k, 4)
                self.landed(self.corner, self.tip_r.at[other], self.tr.at[other])

            loop(3, arrived)
            self.tip_w[...] = self.tip_r[...]
            for i in range(3):
                n = self.nf[4 + self.tip, self.face * 3 + i]
                group = lax.div(jnp.minimum(n, 11), 3)
                got = jnp.where(group == self.face, self.tip_s[0, pl.ds(i, 1)], self.tip_w[group, pl.ds(i, 1)])
                self.cells[self.tip, pl.ds(i, 1)] = jnp.where(n < 12, got, 0.0)

        not_, and_ = jnp.logical_not, jnp.logical_and
        for cell, flat, part, flat_side, upright, up_side in (
            (0, not_(self.left), 0, 3, not_(self.top), 0),
            (1, not_(self.right), 0, 1, not_(self.top), 0),
            (2, not_(self.right), 8, 1, not_(self.bottom), 2),
            (3, not_(self.left), 8, 3, not_(self.bottom), 2),
        ):
            @pl.when(flat)
            def _(cell=cell, part=part, flat_side=flat_side):
                self.cells[cell] = self.end_r[flat_side, pl.ds(part, 8)]

            @pl.when(and_(not_(flat), upright))
            def _(cell=cell, up_side=up_side):
                self.cells[cell] = self.end_r[up_side, pl.ds(0, 8)]

    def copy_end_ok(self, side):
        ok, dev = self.beside(side)
        return jnp.logical_and(ok, jnp.logical_or(lax.rem(side, 2) == 1, self.has_v))

    def wait_sends(self):
        loop(4, lambda k: self.sent(self.copy_beside(k)))
        loop(16, lambda k: self.sent(self.copy_class(k)))
        loop(6, lambda k: self.sent(self.copy_across(k)))
        loop(3, lambda k: self.sent(self.copy_tip(k)))
        loop(4, lambda k: self.sent(self.copy_end(k)))


EXCHANGE_SCRATCH = [
    pltpu.VMEM((2, 8, 3, 64, 128), BF16),
    pltpu.VMEM((2, 2, 4, 3, 64, 128), BF16),
    pltpu.VMEM((2, 2, 4, 3, 64, 128), BF16),
    pltpu.VMEM((2, 4, 8, 128), F32),
    pltpu.VMEM((2, 4, 8, 128), F32),
    pltpu.VMEM((2, 4, 16, 128), F32),
    pltpu.VMEM((2, 4, 16, 128), F32),
    pltpu.VMEM((8, 3, 64, 128), BF16), pltpu.VMEM((2, 4, 3, 64, 128), BF16), pltpu.VMEM((4, 8, 128), F32),
    pltpu.SemaphoreType.DMA((2, 4)), pltpu.SemaphoreType.DMA((2, 4)),
    pltpu.SemaphoreType.DMA((2, 2, 8)), pltpu.SemaphoreType.DMA((2, 8)),
    pltpu.SemaphoreType.DMA((2, 2, 4)), pltpu.SemaphoreType.DMA((2, 2, 4)),
    pltpu.SemaphoreType.DMA((2, 4)), pltpu.SemaphoreType.DMA((2, 4)),
    pltpu.SemaphoreType.DMA((2, 4)), pltpu.SemaphoreType.DMA((2, 4)),
]


PICK_AFTER = 2


def widen(w, out):
    out[...] = jnp.zeros(out.shape, BF16)
    for d in range(3):
        for p in range(2):
            for a in range(3):
                out[pl.ds((a + p) * 384 + d * 128, 128), pl.ds(p * 128, 128)] = w[a, d]


def build(f, img, xc, edges):
    col = lax.broadcasted_iota(jnp.int32, (8, 8, 128), 1)

    def rows(g):
        v = img[f, pl.ds(4 * g, 4)].reshape(8, 64, 128)
        wide = v.astype(F32)
        at = pl.ds(pl.multiple_of(8 * g, 8), 8)
        first = jnp.where(col == 0, edges[0, f, at][:, None, :], wide[:, 0:8])
        last = jnp.where(col == 7, edges[1, f, at][:, None, :], wide[:, 56:64])
        wide = jnp.concatenate([first, wide[:, 8:56], last], axis=1)
        parts = [pltpu.roll(wide, 1, 1).astype(BF16), wide.astype(BF16), pltpu.roll(wide, 63, 1).astype(BF16)]
        for i in range(8):
            k = 1 + i
            for d in range(3):
                xc[f, 4 * g + k // 2, k % 2, :, d * 128:(d + 1) * 128] = parts[d][i]

    loop(8, rows)


def inner(f, xc, w2, bias, img, after):
    def chunk(g):
        lhs = jnp.concatenate(
            [xc[f, pl.ds(PAIRS * g + t // 2, PAIRS), t % 2].reshape(PAIRS * 64, 384) for t in range(4)], axis=1)
        o = gelu(jnp.dot(lhs, w2[...], preferred_element_type=F32) + bias).astype(BF16)
        for p in range(2):
            img[f, pl.ds(PAIRS * g, PAIRS), p] = o[:, p * 128:(p + 1) * 128].reshape(PAIRS, 64, 128)
        after(32 // PAIRS * f + g)

    loop(32 // PAIRS, chunk)


SIDES = ((0, 3, 0, 128, 0), (1, 1, 256, 0, 62))


def ring_ready(f, xc, cols, g, rl, fix):
    for e, r, x0 in ((0, ((0, 1), (1, 0)), 384), (2, ((31, 1), (32, 0)), 0)):
        for k in range(2):
            rl[f, pl.ds(e * 64, 64), pl.ds(x0 + k * 384, 384)] = xc[f, r[k][0], r[k][1]]
    for side, e, rim, own, px in SIDES:
        for k in range(2):
            g[side, pl.ds(1, 64), pl.ds(k * 128, 128)] = cols[2 * side + k, f]
        for a in range(3):
            to = pl.ds(a * 384 + own, 256)
            rl[f, pl.ds(e * 64, 64), to] = g[side, pl.ds(a, 64)].astype(BF16)
            for tip, at in (((0, 1)[side], 0), ((3, 2)[side], 63)):
                fix[f, tip:tip + 1, to] = g[side, a + at:a + at + 1]


def ring(f, halo, rl, fix, w, bias, out):
    for e in range(4):
        mid = halo[e, f]
        wide = mid.astype(F32)
        parts = (pltpu.roll(wide, 1, 0).astype(BF16), mid, pltpu.roll(wide, 63, 0).astype(BF16))
        lane, step = ((0, 128), (256, 384), (768, 128), (0, 384))[e]
        for k in range(3):
            rl[f, pl.ds(e * 64, 64), pl.ds(lane + k * step, 128)] = parts[k]
        if e % 2 == 0:
            a = e * 384
            for side, _, rim, own, px in SIDES:
                tip = ((0, 1), (3, 2))[e // 2][side]
                for k in range(2):
                    fix[f, tip:tip + 1, pl.ds(a + own + k * 128, 128)] = wide[px + k:px + k + 1]
        else:
            for tip, a, at in (((1, 0)[e // 2], 384, 0), ((2, 3)[e // 2], 0, 62)):
                for k in range(2):
                    fix[f, tip:tip + 1, pl.ds(a + lane + k * 384, 128)] = wide[at + k:at + k + 1]
    out[f] = gelu(jnp.dot(rl[f], w, preferred_element_type=F32) + bias)


def corners(cells, fix, w, bias, out):
    for f in range(3):
        for tip, lane in ((0, 0), (1, 256), (2, 768 + 256), (3, 768)):
            fix[f, tip:tip + 1, pl.ds(lane, 128)] = cells[tip, f:f + 1]
    o = gelu(jnp.dot(fix[...].reshape(24, 1152).astype(BF16), w, preferred_element_type=F32) + bias)
    for f in range(3):
        for tip, at in ((0, 192), (1, 64), (2, 127), (3, 255)):
            out[f, at:at + 1] = o[8 * f + tip:8 * f + tip + 1]


def settle(f, o, out, edges):
    row = lax.broadcasted_iota(jnp.int32, (64, 128), 0)
    left, right = o[f, 192:256], o[f, 64:128]
    out[3, f] = left.astype(BF16)
    out[1, f] = right.astype(BF16)
    edges[0, f] = left
    edges[1, f] = right
    for e, k in ((0, 0), (2, 63)):
        line = jnp.where(row == 0, left[k:k + 1], jnp.where(row == 63, right[k:k + 1], o[f, e * 64:(e + 1) * 64]))
        out[e, f] = line.astype(BF16)


def main_kernel(x, nf_in, ori_in, w1, b1, w2, b2, skip, ring_out,
                img, nf, ori, xc, wv, bv, wide, lines, halo, cells, cols, edges, g, rl, fix, rims, load, store, *rest):
    bufs, seen, sems = rest[:7], rest[7:10], rest[10:]

    def exchange(layer):
        return Exchange(lines.at[layer], halo.at[layer], cells.at[layer], nf, ori,
                        *[b.at[layer] for b in bufs], [s.at[layer] for s in sems], seen)

    ends, middle = (pl.ds(0, 16), pl.ds(48, 16)), pl.ds(16, 32)
    moves = [pltpu.make_async_copy(src, dst, load.at[k]) for k, (src, dst) in enumerate((
        (x.at[:, :, :, ends[0]], img.at[:, :, :, ends[0]]), (x.at[:, :, :, ends[1]], img.at[:, :, :, ends[1]]),
        (x.at[:, 0, 0], lines.at[0, 0]), (x.at[:, 31, 1], lines.at[0, 2]),
        (x.at[:, :, :, middle], img.at[:, :, :, middle]),
        (w1, wv.at[0]), (b1, bv.at[0]), (nf_in, nf), (ori_in, ori), (w2, wv.at[1]), (b2, bv.at[1])))]
    for m in moves:
        m.start()
    exchange(0).greet()
    bufs[5][...] = jnp.zeros(bufs[5].shape, F32)
    bufs[3][...] = jnp.zeros(bufs[3].shape, F32)
    cells[...] = jnp.zeros(cells.shape, F32)
    fix[...] = jnp.zeros(fix.shape, F32)
    g[...] = jnp.zeros(g.shape, F32)

    def clear(f):
        xc[f, 0, 0] = jnp.zeros((64, 384), BF16)
        xc[f, 32, 1] = jnp.zeros((64, 384), BF16)

    loop(3, clear)
    for m in moves[:4]:
        m.wait()

    def first(f):
        near = img[f, :, :, 0:16].reshape(64, 16, 128).astype(F32)[:, 0]
        far = img[f, :, :, 48:64].reshape(64, 16, 128).astype(F32)[:, 15]
        edges[0, f] = near
        edges[1, f] = far
        lines[0, 3, f] = near.astype(BF16)
        lines[0, 1, f] = far.astype(BF16)

    loop(3, first)
    exchange(0).greeted()
    out = [pltpu.make_async_copy(img.at[f], skip.at[f], store.at[f]) for f in range(3)]

    def layer(k):
        ex = exchange(k)
        ex.start_a()

        @pl.when(k == 0)
        def _():
            for m in moves[4:]:
                m.wait()

        widen(wv.at[k], wide)
        bias = jnp.concatenate([bv[k], bv[k]], axis=1)

        def prepare(f):
            img[f, 0, 0] = lines[k, 0, f]
            img[f, 31, 1] = lines[k, 2, f]
            cols[0, f] = edges[0, f]
            cols[1, f] = img[f, :, :, 0:16].reshape(64, 16, 128).astype(F32)[:, 1]
            cols[2, f] = img[f, :, :, 48:64].reshape(64, 16, 128).astype(F32)[:, 14]
            cols[3, f] = edges[1, f]
            build(f, img, xc, edges)

        loop(3, prepare)

        def after(chunk):
            @pl.when(chunk == PICK_AFTER)
            def _():
                ex.stage_b()

        def face(f):
            inner(f, xc, wide, bias, img, after)

            @pl.when(k == 1)
            def _():
                pltpu.make_async_copy(img.at[f], skip.at[f], store.at[f]).start()

        loop(3, face)
        loop(3, lambda f: ring_ready(f, xc, cols, g, rl, fix))
        ex.stage_c()
        ex.start_d()
        w = wv[k].reshape(1152, 128)
        loop(3, lambda f: ring(f, halo.at[k], rl, fix, w, bv[k], rims))
        ex.finish()
        corners(cells.at[k], fix, w, bv[k], rims)
        loop(3, lambda f: settle(f, rims, lines.at[k + 1], edges))
        ex.wait_sends()

    loop(2, layer)
    ring_out[...] = lines[2]
    for o in out:
        o.wait()


def main(x, nf, ori, w1, b1, w2, b2):
    vm = pl.BlockSpec(memory_space=pltpu.VMEM)
    hbm = pl.BlockSpec(memory_space=pl.ANY)
    V = pltpu.VMEM
    return pl.pallas_call(
        main_kernel,
        in_specs=[hbm] * 7,
        out_specs=[hbm, vm],
        out_shape=[jax.ShapeDtypeStruct((3, 32, 2, 64, 128), BF16), jax.ShapeDtypeStruct((4, 3, 64, 128), BF16)],
        scratch_shapes=[
            V((3, 32, 2, 64, 128), BF16),
            pltpu.SMEM((8, 12), jnp.int32), pltpu.SMEM((8, 12), jnp.int32),
            V((3, 33, 2, 64, 384), BF16),
            V((2, 3, 3, 128, 128), BF16), V((2, 1, 128), F32),
            V((1536, 256), BF16),
            V((3, 4, 3, 64, 128), BF16), V((2, 4, 3, 64, 128), BF16),
            V((2, 4, 8, 128), F32),
            V((4, 3, 64, 128), F32), V((2, 3, 64, 128), F32),
            V((2, 72, 256), F32), V((3, 256, 1152), BF16),
            V((3, 8, 1152), F32), V((3, 256, 128), F32),
            pltpu.SemaphoreType.DMA((11,)), pltpu.SemaphoreType.DMA((3,)),
        ] + EXCHANGE_SCRATCH,
        compiler_params=pltpu.CompilerParams(collective_id=0, has_side_effects=True, vmem_limit_bytes=58 * 2**20),
    )(x.reshape(3, 32, 2, 64, 128), nf.T, ori.T, w1, b1.reshape(1, 128), w2, b2.reshape(1, 128))


def last_kernel(s, rim, wd_ref, bd_ref, out, coarse, wd, g32):
    f, g = pl.program_id(0), pl.program_id(1)
    P = s.shape[1]

    @pl.when(jnp.logical_and(f == 0, g == 0))
    def _():
        build_wd(wd_ref, wd)

    col = lax.broadcasted_iota(jnp.int32, (2 * P, 8, 128), 1)
    rows = pl.ds(pl.multiple_of(2 * P * g, 16), 2 * P)
    v = s[0].reshape(2 * P, 64, 128)
    wide = v.astype(F32)
    first = jnp.where(col == 0, rim[3, f, rows].astype(F32)[:, None, :], wide[:, 0:8])
    last = jnp.where(col == 7, rim[1, f, rows].astype(F32)[:, None, :], wide[:, 56:64])
    wide = jnp.concatenate([first, wide[:, 8:56], last], axis=1).reshape(P, 2, 64, 128)
    for a in range(2):
        g32[a] = wide[:, a].reshape(P * 64, 128)

    @pl.when(g == 0)
    def _():
        g32[0, 0:64] = rim[0, f].astype(F32)

    @pl.when(g == pl.num_programs(1) - 1)
    def _():
        g32[1, pl.ds((P - 1) * 64, 64)] = rim[2, f].astype(F32)

    for a in range(2):
        out[0, :, a] = g32[a].astype(BF16).reshape(P, 64, 128)
    parts = [g32[a, pl.ds(d, P * 32, stride=2), :] for d in range(2) for a in range(2)]
    q = jnp.concatenate(parts, axis=1).astype(BF16)
    cc = jnp.dot(q, wd[...], preferred_element_type=F32) + bd_ref[...]
    coarse[0] = cc.astype(BF16).reshape(P, 32, 256)


def last(s, rim, wd, bd, P=32):
    full = lambda *shape: pl.BlockSpec(shape, lambda f, g: (0,) * len(shape))
    block = pl.BlockSpec((1, P, 2, 64, 128), lambda f, g: (f, g, 0, 0, 0))
    skip, coarse = pl.pallas_call(
        last_kernel, grid=(3, 32 // P),
        in_specs=[block, full(4, 3, 64, 128), full(2, 2, 128, 256), full(1, 256)],
        out_specs=[block, pl.BlockSpec((1, P, 32, 256), lambda f, g: (f, g, 0, 0))],
        out_shape=[jax.ShapeDtypeStruct((3, 32, 2, 64, 128), BF16), jax.ShapeDtypeStruct((3, 32, 32, 256), BF16)],
        scratch_shapes=[pltpu.VMEM((512, 256), BF16), pltpu.VMEM((2, P * 64, 128), F32)],
        compiler_params=pltpu.CompilerParams(vmem_limit_bytes=58 * 2**20, dimension_semantics=("arbitrary", "arbitrary")),
    )(s, rim, wd, bd.reshape(1, 256))
    return skip.reshape(3, 64, 64, 128), coarse


def per_device(field, conv1_w, conv1_b, conv2_w, conv2_b, down_w, down_b, neighbour_face, orientation):
    s, rim = main(field, neighbour_face, orientation, conv1_w, conv1_b, conv2_w, conv2_b)
    return last(s, rim, down_w, down_b)


def solution(mesh):
    return jax.shard_map(
        per_device, mesh=mesh,
        in_specs=(P("face", "row", "col", None), P(), P(), P(), P(), P(), P(), P(), P()),
        out_specs=(P("face", "row", "col", None), P("face", "row", "col", None)),
        check_vma=False,
    )
```

```python
import jax
import jax.numpy as jnp
from jax import lax
from jax.experimental import pallas as pl
from jax.experimental.pallas import tpu as pltpu
from jax.sharding import PartitionSpec as P

MESH = pl.DeviceIdType.MESH
F32, BF16 = jnp.float32, jnp.bfloat16
PAIRS = 16

COEF = (0.7978842854499817, 0.03633414953947067, -3.302673940197565e-05, -5.5273376347031444e-05, 3.974068931711372e-06, -1.3378310370626423e-07, 1.8139250101967264e-09)

def gelu(v):
    s = jnp.minimum(v * v, 64.0)
    p = COEF[-1] * s + COEF[-2]
    for k in COEF[-3::-1]:
        p = p * s + k
    h = 0.5 * v
    return h + h * jnp.tanh(p * v)

def build_wd(wd_ref, wd):
    for d in range(2):
        for a in range(2):
            wd[pl.ds((d*2+a)*128, 128), :] = wd_ref[a, d]

def loop(count, body):
    def step(k, _):
        body(k)
        return 0

    lax.fori_loop(0, count, step, 0)


class Exchange:
    def __init__(self, lines, halo, cells, nf, ori, pool, send_b, recv_b, tip_s, tip_r, end_s, end_r, sems, seen):
        self.lines, self.halo, self.cells, self.nf, self.ori = lines, halo, cells, nf, ori
        self.pool, self.send_b, self.recv_b = pool, send_b, recv_b
        self.tip_s, self.tip_r, self.end_s, self.end_r = tip_s, tip_r, end_s, end_r
        (self.hs, self.hr, self.as_, self.ar, self.bs, self.br, self.ts, self.tr, self.es, self.er) = sems
        self.pool_w, self.recv_w, self.tip_w = seen
        self.face, self.row, self.col = lax.axis_index("face"), lax.axis_index("row"), lax.axis_index("col")
        self.top, self.bottom = self.row == 0, self.row == 7
        self.left, self.right = self.col == 0, self.col == 7
        self.has_h = jnp.logical_or(self.top, self.bottom)
        self.has_v = jnp.logical_or(self.left, self.right)
        self.corner = jnp.logical_and(self.has_h, self.has_v)
        self.rim = jnp.logical_or(self.has_h, self.has_v)
        self.edge_h = jnp.where(self.top, 0, 2)
        self.edge_v = jnp.where(self.left, 3, 1)
        self.tip = jnp.where(self.top, jnp.where(self.left, 0, 1), jnp.where(self.left, 3, 2))

    def own(self, which):
        flat = which == 0
        has = jnp.logical_or(jnp.logical_and(flat, self.has_h), jnp.logical_and(jnp.logical_not(flat), self.has_v))
        edge = jnp.where(flat, self.edge_h, self.edge_v)
        seg = jnp.where(flat, self.col, self.row)
        return has, edge, seg, edge * 2 + jnp.where(seg >= 4, 1, 0)

    def beside(self, side):
        r = self.row + jnp.where(side == 0, -1, jnp.where(side == 2, 1, 0))
        c = self.col + jnp.where(side == 1, 1, jnp.where(side == 3, -1, 0))
        ok = jnp.logical_and(jnp.logical_and(r >= 0, r <= 7), jnp.logical_and(c >= 0, c <= 7))
        return ok, (self.face, r, c)

    def classmate(self, k):
        which, q = lax.div(k, 8), lax.rem(k, 8)
        has, edge, seg, slot = self.own(which)
        low = jnp.where(seg >= 4, 7 - seg, seg)
        s = jnp.where(lax.rem(q, 2) == 0, low, 7 - low)
        e = lax.div(q, 2)
        r = jnp.where(e == 0, 0, jnp.where(e == 2, 7, s))
        c = jnp.where(e == 1, 7, jnp.where(e == 3, 0, s))
        other = jnp.logical_or(r != self.row, c != self.col)
        once = jnp.logical_or(low > 0, lax.rem(q, 4) < 2)
        return which, q, edge, slot, jnp.logical_and(has, jnp.logical_and(other, once)), (self.face, r, c)

    def across(self, d):
        return (lax.rem(self.face + d, 4), self.row, self.col)

    def greet(self):
        barrier = pltpu.get_barrier_semaphore()

        def meet(ok, dev):
            @pl.when(ok)
            def _():
                pl.semaphore_signal(barrier, inc=1, device_id=dev, device_id_type=MESH)

        loop(4, lambda k: meet(*self.beside(k)))
        loop(16, lambda k: meet(*self.classmate(k)[4:]))
        loop(3, lambda k: meet(self.rim, self.across(k + 1)))

    def greeted(self):
        barrier = pltpu.get_barrier_semaphore()

        near = sum(jnp.where(end, 0, 1) for end in (self.top, self.bottom, self.left, self.right))
        far = jnp.where(self.corner, 9, jnp.where(self.rim, 10, 0))
        pl.semaphore_wait(barrier, near + far)

    def copy_beside(self, side):
        ok, dev = self.beside(side)
        there = lax.rem(side + 2, 4)
        return ok, pltpu.make_async_remote_copy(
            self.lines.at[side], self.halo.at[there], self.hs.at[side], self.hr.at[there],
            device_id=dev, device_id_type=MESH)

    def copy_class(self, k):
        which, q, edge, slot, ok, dev = self.classmate(k)
        return ok, pltpu.make_async_remote_copy(
            self.lines.at[edge], self.pool.at[slot], self.as_.at[which, q], self.ar.at[slot],
            device_id=dev, device_id_type=MESH)

    def copy_across(self, k):
        which, d = lax.div(k, 3), lax.rem(k, 3) + 1
        return self.own(which)[0], pltpu.make_async_remote_copy(
            self.send_b.at[which, d], self.recv_b.at[which, self.face], self.bs.at[which, d],
            self.br.at[which, self.face], device_id=self.across(d), device_id_type=MESH)

    def copy_tip(self, k):
        d = k + 1
        return self.corner, pltpu.make_async_remote_copy(
            self.tip_s.at[d], self.tip_r.at[self.face], self.ts.at[d], self.tr.at[self.face],
            device_id=self.across(d), device_id_type=MESH)

    def copy_end(self, side):
        ok, dev = self.beside(side)
        there = lax.rem(side + 2, 4)
        ok = jnp.logical_and(ok, jnp.logical_or(lax.rem(side, 2) == 1, self.has_v))
        return ok, pltpu.make_async_remote_copy(
            self.end_s.at[side], self.end_r.at[there], self.es.at[side], self.er.at[there],
            device_id=dev, device_id_type=MESH)

    @staticmethod
    def start(pair):
        ok, copy = pair

        @pl.when(ok)
        def _():
            copy.start()

    @staticmethod
    def sent(pair):
        ok, copy = pair

        @pl.when(ok)
        def _():
            copy.wait_send()

    @staticmethod
    def landed(ok, dst, sem):
        @pl.when(ok)
        def _():
            pltpu.make_async_copy(dst, dst, sem).wait()

    def start_a(self):
        loop(16, lambda k: self.start(self.copy_class(k)))
        loop(4, lambda k: self.start(self.copy_beside(k)))

        def keep(which):
            has, edge, seg, slot = self.own(which)

            @pl.when(has)
            def _():
                self.pool[slot] = self.lines[edge]

        loop(2, keep)

    def picked(self, which, face, i):
        has, edge, seg, slot = self.own(which)
        n, o = self.nf[edge, face * 3 + i], self.ori[edge, face * 3 + i]
        side, turned = lax.div(o, 2), lax.rem(o, 2)
        s = jnp.where(turned == 1, 7 - seg, seg)
        return self.pool_w[side * 2 + jnp.where(s >= 4, 1, 0), lax.rem(n, 3)]

    def picked_tip(self, face, i):
        n, k = jnp.minimum(self.nf[4 + self.tip, face * 3 + i], 11), self.ori[4 + self.tip, face * 3 + i]
        line = self.pool_w[jnp.where(k == 2, 5, jnp.where(k == 3, 4, k)), lax.rem(n, 3)].astype(F32)
        return jnp.where(jnp.logical_or(k == 1, k == 2), line[63:64], line[0:1])

    def stage_b(self):
        @pl.when(self.rim)
        def _():
            slot_h, slot_v = self.own(0)[3], self.own(1)[3]

            def arrived(q):
                mine = jnp.logical_or(
                    jnp.logical_and(self.has_h, slot_h == q), jnp.logical_and(self.has_v, slot_v == q))
                self.landed(jnp.logical_not(mine), self.pool.at[q], self.ar.at[q])

            loop(8, arrived)

            def take(q):
                self.pool_w[q] = self.pool[q]

            loop(8, take)

            def pick(k):
                at = lax.rem(k, 4)
                which, d = lax.div(k, 4), jnp.where(at == 0, 2, jnp.where(at == 1, 1, jnp.where(at == 2, 3, 0)))

                @pl.when(self.own(which)[0])
                def _():
                    for i in range(3):
                        self.send_b[which, d, i] = self.picked(which, self.across(d)[0], i)

                    @pl.when(d > 0)
                    def _():
                        self.copy_across(which * 3 + jnp.maximum(d - 1, 0))[1].start()

            loop(8, pick)

            @pl.when(self.corner)
            def _():
                def tips(k):
                    d = lax.rem(k + 1, 4)
                    for i in range(3):
                        self.tip_s[d, pl.ds(i, 1)] = self.picked_tip(self.across(d)[0], i)

                    @pl.when(d > 0)
                    def _():
                        self.copy_tip(jnp.maximum(d - 1, 0))[1].start()

                loop(4, tips)

    def stage_c(self):
        def arrived(k):
            which, other = lax.div(k, 3), lax.rem(self.face + 1 + lax.rem(k, 3), 4)
            self.landed(self.own(which)[0], self.recv_b.at[which, other], self.br.at[which, other])

        loop(6, arrived)

        def take(k):
            which, group = lax.div(k, 4), lax.rem(k, 4)
            has = self.own(which)[0]

            @pl.when(jnp.logical_and(has, group != self.face))
            def _():
                self.recv_w[which, group] = self.recv_b[which, group]

        loop(8, take)
        i0 = lax.broadcasted_iota(jnp.int32, (64, 64), 0)
        i1 = lax.broadcasted_iota(jnp.int32, (64, 64), 1)

        def turn(k):
            which, i = lax.div(k, 3), lax.rem(k, 3)
            has, edge, seg, slot = self.own(which)

            @pl.when(has)
            def _():
                n, o = self.nf[edge, self.face * 3 + i], self.ori[edge, self.face * 3 + i]
                group = lax.div(n, 3)
                order = jnp.where(i1 == jnp.where(lax.rem(o, 2) == 1, 63 - i0, i0), 1.0, 0.0).astype(BF16)
                line = jnp.where(group == self.face, self.send_b[which, 0, i], self.recv_w[which, group, i])
                self.halo[edge, i] = jnp.dot(order, line, preferred_element_type=F32).astype(BF16)

        loop(6, turn)
        loop(4, lambda k: self.landed(self.beside(k)[0], self.halo.at[k], self.hr.at[k]))

    def start_d(self):
        def ends(side):
            last = jnp.logical_or(side == 1, side == 2)
            for i in range(3):
                for part, line in ((0, jnp.where(lax.rem(side, 2) == 1, 0, self.edge_v)), (8, 2)):
                    v = self.halo[line, i].astype(F32)
                    self.end_s[side, pl.ds(part + i, 1)] = jnp.where(last, v[63:64], v[0:1])

            self.start(self.copy_end(side))

        loop(4, ends)

    def finish(self):
        loop(4, lambda k: self.landed(self.copy_end_ok(k), self.end_r.at[k], self.er.at[k]))

        @pl.when(self.corner)
        def _():
            def arrived(k):
                other = lax.rem(self.face + 1 + k, 4)
                self.landed(self.corner, self.tip_r.at[other], self.tr.at[other])

            loop(3, arrived)
            self.tip_w[...] = self.tip_r[...]
            for i in range(3):
                n = self.nf[4 + self.tip, self.face * 3 + i]
                group = lax.div(jnp.minimum(n, 11), 3)
                got = jnp.where(group == self.face, self.tip_s[0, pl.ds(i, 1)], self.tip_w[group, pl.ds(i, 1)])
                self.cells[self.tip, pl.ds(i, 1)] = jnp.where(n < 12, got, 0.0)

        not_, and_ = jnp.logical_not, jnp.logical_and
        for cell, flat, part, flat_side, upright, up_side in (
            (0, not_(self.left), 0, 3, not_(self.top), 0),
            (1, not_(self.right), 0, 1, not_(self.top), 0),
            (2, not_(self.right), 8, 1, not_(self.bottom), 2),
            (3, not_(self.left), 8, 3, not_(self.bottom), 2),
        ):
            @pl.when(flat)
            def _(cell=cell, part=part, flat_side=flat_side):
                self.cells[cell] = self.end_r[flat_side, pl.ds(part, 8)]

            @pl.when(and_(not_(flat), upright))
            def _(cell=cell, up_side=up_side):
                self.cells[cell] = self.end_r[up_side, pl.ds(0, 8)]

    def copy_end_ok(self, side):
        ok, dev = self.beside(side)
        return jnp.logical_and(ok, jnp.logical_or(lax.rem(side, 2) == 1, self.has_v))

    def wait_sends_a(self):
        loop(4, lambda k: self.sent(self.copy_beside(k)))
        loop(16, lambda k: self.sent(self.copy_class(k)))

    def wait_sends(self):
        loop(6, lambda k: self.sent(self.copy_across(k)))
        loop(3, lambda k: self.sent(self.copy_tip(k)))
        loop(4, lambda k: self.sent(self.copy_end(k)))


EXCHANGE_SCRATCH = [
    pltpu.VMEM((2, 8, 3, 64, 128), BF16),
    pltpu.VMEM((2, 2, 4, 3, 64, 128), BF16),
    pltpu.VMEM((2, 2, 4, 3, 64, 128), BF16),
    pltpu.VMEM((2, 4, 8, 128), F32),
    pltpu.VMEM((2, 4, 8, 128), F32),
    pltpu.VMEM((2, 4, 16, 128), F32),
    pltpu.VMEM((2, 4, 16, 128), F32),
    pltpu.VMEM((8, 3, 64, 128), BF16), pltpu.VMEM((2, 4, 3, 64, 128), BF16), pltpu.VMEM((4, 8, 128), F32),
    pltpu.SemaphoreType.DMA((2, 4)), pltpu.SemaphoreType.DMA((2, 4)),
    pltpu.SemaphoreType.DMA((2, 2, 8)), pltpu.SemaphoreType.DMA((2, 8)),
    pltpu.SemaphoreType.DMA((2, 2, 4)), pltpu.SemaphoreType.DMA((2, 2, 4)),
    pltpu.SemaphoreType.DMA((2, 4)), pltpu.SemaphoreType.DMA((2, 4)),
    pltpu.SemaphoreType.DMA((2, 4)), pltpu.SemaphoreType.DMA((2, 4)),
]


PICK_AFTER = 2


def widen(w, out):
    out[...] = jnp.zeros(out.shape, BF16)
    for d in range(3):
        for p in range(2):
            for a in range(3):
                out[pl.ds((a + p) * 384 + d * 128, 128), pl.ds(p * 128, 128)] = w[a, d]


def build(f, img, xc, edges):
    col = lax.broadcasted_iota(jnp.int32, (8, 8, 128), 1)

    def rows(g):
        v = img[f, pl.ds(4 * g, 4)].reshape(8, 64, 128)
        wide = v.astype(F32)
        at = pl.ds(pl.multiple_of(8 * g, 8), 8)
        first = jnp.where(col == 0, edges[0, f, at][:, None, :], wide[:, 0:8])
        last = jnp.where(col == 7, edges[1, f, at][:, None, :], wide[:, 56:64])
        wide = jnp.concatenate([first, wide[:, 8:56], last], axis=1)
        parts = [pltpu.roll(wide, 1, 1).astype(BF16), wide.astype(BF16), pltpu.roll(wide, 63, 1).astype(BF16)]
        for i in range(8):
            k = 1 + i
            for d in range(3):
                xc[f, 4 * g + k // 2, k % 2, :, d * 128:(d + 1) * 128] = parts[d][i]

    loop(8, rows)


def inner(f, xc, w2, bias, img, after):
    def chunk(g):
        lhs = jnp.concatenate(
            [xc[f, pl.ds(PAIRS * g + t // 2, PAIRS), t % 2].reshape(PAIRS * 64, 384) for t in range(4)], axis=1)
        o = gelu(jnp.dot(lhs, w2[...], preferred_element_type=F32) + bias).astype(BF16)
        for p in range(2):
            img[f, pl.ds(PAIRS * g, PAIRS), p] = o[:, p * 128:(p + 1) * 128].reshape(PAIRS, 64, 128)
        after(32 // PAIRS * f + g)

    loop(32 // PAIRS, chunk)


SIDES = ((0, 3, 0, 128, 0), (1, 1, 256, 0, 62))


def ring_ready(f, xc, cols, g, rl, fix):
    for e, r, x0 in ((0, ((0, 1), (1, 0)), 384), (2, ((31, 1), (32, 0)), 0)):
        for k in range(2):
            rl[f, pl.ds(e * 64, 64), pl.ds(x0 + k * 384, 384)] = xc[f, r[k][0], r[k][1]]
    for side, e, rim, own, px in SIDES:
        for k in range(2):
            g[side, pl.ds(1, 64), pl.ds(k * 128, 128)] = cols[2 * side + k, f]
        for a in range(3):
            to = pl.ds(a * 384 + own, 256)
            rl[f, pl.ds(e * 64, 64), to] = g[side, pl.ds(a, 64)].astype(BF16)
            for tip, at in (((0, 1)[side], 0), ((3, 2)[side], 63)):
                fix[f, tip:tip + 1, to] = g[side, a + at:a + at + 1]


def ring(f, halo, rl, fix, w, bias, out):
    for e in range(4):
        mid = halo[e, f]
        wide = mid.astype(F32)
        parts = (pltpu.roll(wide, 1, 0).astype(BF16), mid, pltpu.roll(wide, 63, 0).astype(BF16))
        lane, step = ((0, 128), (256, 384), (768, 128), (0, 384))[e]
        for k in range(3):
            rl[f, pl.ds(e * 64, 64), pl.ds(lane + k * step, 128)] = parts[k]
        if e % 2 == 0:
            a = e * 384
            for side, _, rim, own, px in SIDES:
                tip = ((0, 1), (3, 2))[e // 2][side]
                for k in range(2):
                    fix[f, tip:tip + 1, pl.ds(a + own + k * 128, 128)] = wide[px + k:px + k + 1]
        else:
            for tip, a, at in (((1, 0)[e // 2], 384, 0), ((2, 3)[e // 2], 0, 62)):
                for k in range(2):
                    fix[f, tip:tip + 1, pl.ds(a + lane + k * 384, 128)] = wide[at + k:at + k + 1]
    out[f] = gelu(jnp.dot(rl[f], w, preferred_element_type=F32) + bias)


def corners(cells, fix, w, bias, out):
    for f in range(3):
        for tip, lane in ((0, 0), (1, 256), (2, 768 + 256), (3, 768)):
            fix[f, tip:tip + 1, pl.ds(lane, 128)] = cells[tip, f:f + 1]
    o = gelu(jnp.dot(fix[...].reshape(24, 1152).astype(BF16), w, preferred_element_type=F32) + bias)
    for f in range(3):
        for tip, at in ((0, 192), (1, 64), (2, 127), (3, 255)):
            out[f, at:at + 1] = o[8 * f + tip:8 * f + tip + 1]


def settle(f, o, out, edges):
    row = lax.broadcasted_iota(jnp.int32, (64, 128), 0)
    left, right = o[f, 192:256], o[f, 64:128]
    out[3, f] = left.astype(BF16)
    out[1, f] = right.astype(BF16)
    edges[0, f] = left
    edges[1, f] = right
    for e, k in ((0, 0), (2, 63)):
        line = jnp.where(row == 0, left[k:k + 1], jnp.where(row == 63, right[k:k + 1], o[f, e * 64:(e + 1) * 64]))
        out[e, f] = line.astype(BF16)


def main_kernel(x, nf_in, ori_in, w1, b1, w2, b2, skip, ring_out,
                img, nf, ori, xc, wv, bv, wide, lines, halo, cells, cols, edges, g, rl, fix, rims, load, store, *rest):
    bufs, seen, sems = rest[:7], rest[7:10], rest[10:]

    def exchange(layer):
        return Exchange(lines.at[layer], halo.at[layer], cells.at[layer], nf, ori,
                        *[b.at[layer] for b in bufs], [s.at[layer] for s in sems], seen)

    ends, middle = (pl.ds(0, 16), pl.ds(48, 16)), pl.ds(16, 32)
    moves = [pltpu.make_async_copy(src, dst, load.at[k]) for k, (src, dst) in enumerate((
        (x.at[:, :, :, ends[0]], img.at[:, :, :, ends[0]]), (x.at[:, :, :, ends[1]], img.at[:, :, :, ends[1]]),
        (x.at[:, 0, 0], lines.at[0, 0]), (x.at[:, 31, 1], lines.at[0, 2]),
        (x.at[:, :, :, middle], img.at[:, :, :, middle]),
        (w1, wv.at[0]), (b1, bv.at[0]), (nf_in, nf), (ori_in, ori), (w2, wv.at[1]), (b2, bv.at[1])))]
    for m in moves:
        m.start()
    exchange(0).greet()
    bufs[5][...] = jnp.zeros(bufs[5].shape, F32)
    bufs[3][...] = jnp.zeros(bufs[3].shape, F32)
    cells[...] = jnp.zeros(cells.shape, F32)
    fix[...] = jnp.zeros(fix.shape, F32)
    g[...] = jnp.zeros(g.shape, F32)

    def clear(f):
        xc[f, 0, 0] = jnp.zeros((64, 384), BF16)
        xc[f, 32, 1] = jnp.zeros((64, 384), BF16)

    loop(3, clear)
    for m in moves[:4]:
        m.wait()

    def first(f):
        near = img[f, :, :, 0:16].reshape(64, 16, 128).astype(F32)[:, 0]
        far = img[f, :, :, 48:64].reshape(64, 16, 128).astype(F32)[:, 15]
        edges[0, f] = near
        edges[1, f] = far
        lines[0, 3, f] = near.astype(BF16)
        lines[0, 1, f] = far.astype(BF16)

    loop(3, first)
    exchange(0).greeted()
    out = [pltpu.make_async_copy(img.at[f], skip.at[f], store.at[f]) for f in range(3)]

    def layer(k):
        ex = exchange(k)
        ex.start_a()

        @pl.when(k == 0)
        def _():
            for m in moves[4:]:
                m.wait()

        widen(wv.at[k], wide)
        bias = jnp.concatenate([bv[k], bv[k]], axis=1)

        def prepare(f):
            img[f, 0, 0] = lines[k, 0, f]
            img[f, 31, 1] = lines[k, 2, f]
            cols[0, f] = edges[0, f]
            cols[1, f] = img[f, :, :, 0:16].reshape(64, 16, 128).astype(F32)[:, 1]
            cols[2, f] = img[f, :, :, 48:64].reshape(64, 16, 128).astype(F32)[:, 14]
            cols[3, f] = edges[1, f]
            build(f, img, xc, edges)

        loop(3, prepare)

        def after(chunk):
            @pl.when(chunk == PICK_AFTER)
            def _():
                ex.stage_b()

        def face(f):
            inner(f, xc, wide, bias, img, after)

            @pl.when(k == 1)
            def _():
                pltpu.make_async_copy(img.at[f], skip.at[f], store.at[f]).start()

        loop(3, face)
        loop(3, lambda f: ring_ready(f, xc, cols, g, rl, fix))
        ex.wait_sends_a()
        ex.stage_c()
        ex.start_d()
        w = wv[k].reshape(1152, 128)
        loop(3, lambda f: ring(f, halo.at[k], rl, fix, w, bv[k], rims))
        ex.finish()
        corners(cells.at[k], fix, w, bv[k], rims)
        loop(3, lambda f: settle(f, rims, lines.at[k + 1], edges))
        ex.wait_sends()

    loop(2, layer)
    ring_out[...] = lines[2]
    for o in out:
        o.wait()


def main(x, nf, ori, w1, b1, w2, b2):
    vm = pl.BlockSpec(memory_space=pltpu.VMEM)
    hbm = pl.BlockSpec(memory_space=pl.ANY)
    V = pltpu.VMEM
    return pl.pallas_call(
        main_kernel,
        in_specs=[hbm] * 7,
        out_specs=[hbm, vm],
        out_shape=[jax.ShapeDtypeStruct((3, 32, 2, 64, 128), BF16), jax.ShapeDtypeStruct((4, 3, 64, 128), BF16)],
        scratch_shapes=[
            V((3, 32, 2, 64, 128), BF16),
            pltpu.SMEM((8, 12), jnp.int32), pltpu.SMEM((8, 12), jnp.int32),
            V((3, 33, 2, 64, 384), BF16),
            V((2, 3, 3, 128, 128), BF16), V((2, 1, 128), F32),
            V((1536, 256), BF16),
            V((3, 4, 3, 64, 128), BF16), V((2, 4, 3, 64, 128), BF16),
            V((2, 4, 8, 128), F32),
            V((4, 3, 64, 128), F32), V((2, 3, 64, 128), F32),
            V((2, 72, 256), F32), V((3, 256, 1152), BF16),
            V((3, 8, 1152), F32), V((3, 256, 128), F32),
            pltpu.SemaphoreType.DMA((11,)), pltpu.SemaphoreType.DMA((3,)),
        ] + EXCHANGE_SCRATCH,
        compiler_params=pltpu.CompilerParams(collective_id=0, has_side_effects=True, vmem_limit_bytes=58 * 2**20),
    )(x.reshape(3, 32, 2, 64, 128), nf.T, ori.T, w1, b1.reshape(1, 128), w2, b2.reshape(1, 128))


def last_kernel(s, rim, wd_ref, bd_ref, out, coarse, wd, g32):
    f, g = pl.program_id(0), pl.program_id(1)
    P = s.shape[1]

    @pl.when(jnp.logical_and(f == 0, g == 0))
    def _():
        build_wd(wd_ref, wd)

    col = lax.broadcasted_iota(jnp.int32, (2 * P, 8, 128), 1)
    rows = pl.ds(pl.multiple_of(2 * P * g, 16), 2 * P)
    v = s[0].reshape(2 * P, 64, 128)
    wide = v.astype(F32)
    first = jnp.where(col == 0, rim[3, f, rows].astype(F32)[:, None, :], wide[:, 0:8])
    last = jnp.where(col == 7, rim[1, f, rows].astype(F32)[:, None, :], wide[:, 56:64])
    wide = jnp.concatenate([first, wide[:, 8:56], last], axis=1).reshape(P, 2, 64, 128)
    for a in range(2):
        g32[a] = wide[:, a].reshape(P * 64, 128)

    @pl.when(g == 0)
    def _():
        g32[0, 0:64] = rim[0, f].astype(F32)

    @pl.when(g == pl.num_programs(1) - 1)
    def _():
        g32[1, pl.ds((P - 1) * 64, 64)] = rim[2, f].astype(F32)

    for a in range(2):
        out[0, :, a] = g32[a].astype(BF16).reshape(P, 64, 128)
    parts = [g32[a, pl.ds(d, P * 32, stride=2), :] for d in range(2) for a in range(2)]
    q = jnp.concatenate(parts, axis=1).astype(BF16)
    cc = jnp.dot(q, wd[...], preferred_element_type=F32) + bd_ref[...]
    coarse[0] = cc.astype(BF16).reshape(P, 32, 256)


def last(s, rim, wd, bd, P=32):
    full = lambda *shape: pl.BlockSpec(shape, lambda f, g: (0,) * len(shape))
    block = pl.BlockSpec((1, P, 2, 64, 128), lambda f, g: (f, g, 0, 0, 0))
    skip, coarse = pl.pallas_call(
        last_kernel, grid=(3, 32 // P),
        in_specs=[block, full(4, 3, 64, 128), full(2, 2, 128, 256), full(1, 256)],
        out_specs=[block, pl.BlockSpec((1, P, 32, 256), lambda f, g: (f, g, 0, 0))],
        out_shape=[jax.ShapeDtypeStruct((3, 32, 2, 64, 128), BF16), jax.ShapeDtypeStruct((3, 32, 32, 256), BF16)],
        scratch_shapes=[pltpu.VMEM((512, 256), BF16), pltpu.VMEM((2, P * 64, 128), F32)],
        compiler_params=pltpu.CompilerParams(vmem_limit_bytes=58 * 2**20, dimension_semantics=("arbitrary", "arbitrary")),
    )(s, rim, wd, bd.reshape(1, 256))
    return skip.reshape(3, 64, 64, 128), coarse


def per_device(field, conv1_w, conv1_b, conv2_w, conv2_b, down_w, down_b, neighbour_face, orientation):
    s, rim = main(field, neighbour_face, orientation, conv1_w, conv1_b, conv2_w, conv2_b)
    return last(s, rim, down_w, down_b)


def solution(mesh):
    return jax.shard_map(
        per_device, mesh=mesh,
        in_specs=(P("face", "row", "col", None), P(), P(), P(), P(), P(), P(), P(), P()),
        out_specs=(P("face", "row", "col", None), P("face", "row", "col", None)),
        check_vma=False,
    )
```

```python
import jax
import jax.numpy as jnp
from jax import lax
from jax.experimental import pallas as pl
from jax.experimental.pallas import tpu as pltpu
from jax.sharding import PartitionSpec as P

MESH = pl.DeviceIdType.MESH
F32, BF16 = jnp.float32, jnp.bfloat16
PAIRS = 16

COEF = (0.7978842854499817, 0.03633414953947067, -3.302673940197565e-05, -5.5273376347031444e-05, 3.974068931711372e-06, -1.3378310370626423e-07, 1.8139250101967264e-09)

def gelu(v):
    s = jnp.minimum(v * v, 64.0)
    p = COEF[-1] * s + COEF[-2]
    for k in COEF[-3::-1]:
        p = p * s + k
    h = 0.5 * v
    return h + h * jnp.tanh(p * v)

def build_wd(wd_ref, wd):
    for d in range(2):
        for a in range(2):
            wd[pl.ds((d*2+a)*128, 128), :] = wd_ref[a, d]

def loop(count, body):
    def step(k, _):
        body(k)
        return 0

    lax.fori_loop(0, count, step, 0)


class Exchange:
    def __init__(self, lines, halo, cells, nf, ori, pool, send_b, recv_b, tip_s, tip_r, end_s, end_r, sems, seen):
        self.lines, self.halo, self.cells, self.nf, self.ori = lines, halo, cells, nf, ori
        self.pool, self.send_b, self.recv_b = pool, send_b, recv_b
        self.tip_s, self.tip_r, self.end_s, self.end_r = tip_s, tip_r, end_s, end_r
        (self.hs, self.hr, self.as_, self.ar, self.bs, self.br, self.ts, self.tr, self.es, self.er) = sems
        self.pool_w, self.recv_w, self.tip_w = seen
        self.face, self.row, self.col = lax.axis_index("face"), lax.axis_index("row"), lax.axis_index("col")
        self.top, self.bottom = self.row == 0, self.row == 7
        self.left, self.right = self.col == 0, self.col == 7
        self.has_h = jnp.logical_or(self.top, self.bottom)
        self.has_v = jnp.logical_or(self.left, self.right)
        self.corner = jnp.logical_and(self.has_h, self.has_v)
        self.rim = jnp.logical_or(self.has_h, self.has_v)
        self.edge_h = jnp.where(self.top, 0, 2)
        self.edge_v = jnp.where(self.left, 3, 1)
        self.tip = jnp.where(self.top, jnp.where(self.left, 0, 1), jnp.where(self.left, 3, 2))

    def own(self, which):
        flat = which == 0
        has = jnp.logical_or(jnp.logical_and(flat, self.has_h), jnp.logical_and(jnp.logical_not(flat), self.has_v))
        edge = jnp.where(flat, self.edge_h, self.edge_v)
        seg = jnp.where(flat, self.col, self.row)
        return has, edge, seg, edge * 2 + jnp.where(seg >= 4, 1, 0)

    def beside(self, side):
        r = self.row + jnp.where(side == 0, -1, jnp.where(side == 2, 1, 0))
        c = self.col + jnp.where(side == 1, 1, jnp.where(side == 3, -1, 0))
        ok = jnp.logical_and(jnp.logical_and(r >= 0, r <= 7), jnp.logical_and(c >= 0, c <= 7))
        return ok, (self.face, r, c)

    def classmate(self, k):
        which, q = lax.div(k, 8), lax.rem(k, 8)
        has, edge, seg, slot = self.own(which)
        low = jnp.where(seg >= 4, 7 - seg, seg)
        s = jnp.where(lax.rem(q, 2) == 0, low, 7 - low)
        e = lax.div(q, 2)
        r = jnp.where(e == 0, 0, jnp.where(e == 2, 7, s))
        c = jnp.where(e == 1, 7, jnp.where(e == 3, 0, s))
        other = jnp.logical_or(r != self.row, c != self.col)
        once = jnp.logical_or(low > 0, lax.rem(q, 4) < 2)
        return which, q, edge, slot, jnp.logical_and(has, jnp.logical_and(other, once)), (self.face, r, c)

    def across(self, d):
        return (lax.rem(self.face + d, 4), self.row, self.col)

    def greet(self):
        barrier = pltpu.get_barrier_semaphore()

        def meet(ok, dev):
            @pl.when(ok)
            def _():
                pl.semaphore_signal(barrier, inc=1, device_id=dev, device_id_type=MESH)

        loop(4, lambda k: meet(*self.beside(k)))
        loop(16, lambda k: meet(*self.classmate(k)[4:]))
        loop(3, lambda k: meet(self.rim, self.across(k + 1)))

    def greeted(self):
        barrier = pltpu.get_barrier_semaphore()

        near = sum(jnp.where(end, 0, 1) for end in (self.top, self.bottom, self.left, self.right))
        far = jnp.where(self.corner, 9, jnp.where(self.rim, 10, 0))
        pl.semaphore_wait(barrier, near + far)

    def copy_beside(self, side):
        ok, dev = self.beside(side)
        there = lax.rem(side + 2, 4)
        return ok, pltpu.make_async_remote_copy(
            self.lines.at[side], self.halo.at[there], self.hs.at[side], self.hr.at[there],
            device_id=dev, device_id_type=MESH)

    def copy_class(self, k):
        which, q, edge, slot, ok, dev = self.classmate(k)
        return ok, pltpu.make_async_remote_copy(
            self.lines.at[edge], self.pool.at[slot], self.as_.at[which, q], self.ar.at[slot],
            device_id=dev, device_id_type=MESH)

    def copy_across(self, k):
        which, d = lax.div(k, 3), lax.rem(k, 3) + 1
        return self.own(which)[0], pltpu.make_async_remote_copy(
            self.send_b.at[which, d], self.recv_b.at[which, self.face], self.bs.at[which, d],
            self.br.at[which, self.face], device_id=self.across(d), device_id_type=MESH)

    def copy_tip(self, k):
        d = k + 1
        return self.corner, pltpu.make_async_remote_copy(
            self.tip_s.at[d], self.tip_r.at[self.face], self.ts.at[d], self.tr.at[self.face],
            device_id=self.across(d), device_id_type=MESH)

    def copy_end(self, side):
        ok, dev = self.beside(side)
        there = lax.rem(side + 2, 4)
        ok = jnp.logical_and(ok, jnp.logical_or(lax.rem(side, 2) == 1, self.has_v))
        return ok, pltpu.make_async_remote_copy(
            self.end_s.at[side], self.end_r.at[there], self.es.at[side], self.er.at[there],
            device_id=dev, device_id_type=MESH)

    @staticmethod
    def start(pair):
        ok, copy = pair

        @pl.when(ok)
        def _():
            copy.start()

    @staticmethod
    def sent(pair):
        ok, copy = pair

        @pl.when(ok)
        def _():
            copy.wait_send()

    @staticmethod
    def landed(ok, dst, sem):
        @pl.when(ok)
        def _():
            pltpu.make_async_copy(dst, dst, sem).wait()

    def start_a(self):
        loop(16, lambda k: self.start(self.copy_class(k)))
        loop(4, lambda k: self.start(self.copy_beside(k)))

        def keep(which):
            has, edge, seg, slot = self.own(which)

            @pl.when(has)
            def _():
                self.pool[slot] = self.lines[edge]

        loop(2, keep)

    def picked(self, which, face, i):
        has, edge, seg, slot = self.own(which)
        n, o = self.nf[edge, face * 3 + i], self.ori[edge, face * 3 + i]
        side, turned = lax.div(o, 2), lax.rem(o, 2)
        s = jnp.where(turned == 1, 7 - seg, seg)
        return self.pool_w[side * 2 + jnp.where(s >= 4, 1, 0), lax.rem(n, 3)]

    def picked_tip(self, face, i):
        n, k = jnp.minimum(self.nf[4 + self.tip, face * 3 + i], 11), self.ori[4 + self.tip, face * 3 + i]
        line = self.pool_w[jnp.where(k == 2, 5, jnp.where(k == 3, 4, k)), lax.rem(n, 3)].astype(F32)
        return jnp.where(jnp.logical_or(k == 1, k == 2), line[63:64], line[0:1])

    def stage_b(self):
        @pl.when(self.rim)
        def _():
            slot_h, slot_v = self.own(0)[3], self.own(1)[3]

            def arrived(q):
                mine = jnp.logical_or(
                    jnp.logical_and(self.has_h, slot_h == q), jnp.logical_and(self.has_v, slot_v == q))
                self.landed(jnp.logical_not(mine), self.pool.at[q], self.ar.at[q])

            loop(8, arrived)

            def take(q):
                self.pool_w[q] = self.pool[q]

            loop(8, take)

            def pick(k):
                at = lax.rem(k, 4)
                which, d = lax.div(k, 4), jnp.where(at == 0, 2, jnp.where(at == 1, 1, jnp.where(at == 2, 3, 0)))

                @pl.when(self.own(which)[0])
                def _():
                    for i in range(3):
                        self.send_b[which, d, i] = self.picked(which, self.across(d)[0], i)

                    @pl.when(d > 0)
                    def _():
                        self.copy_across(which * 3 + jnp.maximum(d - 1, 0))[1].start()

            loop(8, pick)

            @pl.when(self.corner)
            def _():
                def tips(k):
                    d = lax.rem(k + 1, 4)
                    for i in range(3):
                        self.tip_s[d, pl.ds(i, 1)] = self.picked_tip(self.across(d)[0], i)

                    @pl.when(d > 0)
                    def _():
                        self.copy_tip(jnp.maximum(d - 1, 0))[1].start()

                loop(4, tips)

    def stage_c(self):
        def arrived(k):
            which, other = lax.div(k, 3), lax.rem(self.face + 1 + lax.rem(k, 3), 4)
            self.landed(self.own(which)[0], self.recv_b.at[which, other], self.br.at[which, other])

        loop(6, arrived)

        def take(k):
            which, group = lax.div(k, 4), lax.rem(k, 4)
            has = self.own(which)[0]

            @pl.when(jnp.logical_and(has, group != self.face))
            def _():
                self.recv_w[which, group] = self.recv_b[which, group]

        loop(8, take)
        i0 = lax.broadcasted_iota(jnp.int32, (64, 64), 0)
        i1 = lax.broadcasted_iota(jnp.int32, (64, 64), 1)

        def turn(k):
            which, i = lax.div(k, 3), lax.rem(k, 3)
            has, edge, seg, slot = self.own(which)

            @pl.when(has)
            def _():
                n, o = self.nf[edge, self.face * 3 + i], self.ori[edge, self.face * 3 + i]
                group = lax.div(n, 3)
                order = jnp.where(i1 == jnp.where(lax.rem(o, 2) == 1, 63 - i0, i0), 1.0, 0.0).astype(BF16)
                line = jnp.where(group == self.face, self.send_b[which, 0, i], self.recv_w[which, group, i])
                self.halo[edge, i] = jnp.dot(order, line, preferred_element_type=F32).astype(BF16)

        loop(6, turn)
        loop(4, lambda k: self.landed(self.beside(k)[0], self.halo.at[k], self.hr.at[k]))

    def start_d(self):
        def ends(side):
            last = jnp.logical_or(side == 1, side == 2)
            for i in range(3):
                for part, line in ((0, jnp.where(lax.rem(side, 2) == 1, 0, self.edge_v)), (8, 2)):
                    v = self.halo[line, i].astype(F32)
                    self.end_s[side, pl.ds(part + i, 1)] = jnp.where(last, v[63:64], v[0:1])

            self.start(self.copy_end(side))

        loop(4, ends)

    def finish(self):
        loop(4, lambda k: self.landed(self.copy_end_ok(k), self.end_r.at[k], self.er.at[k]))

        @pl.when(self.corner)
        def _():
            def arrived(k):
                other = lax.rem(self.face + 1 + k, 4)
                self.landed(self.corner, self.tip_r.at[other], self.tr.at[other])

            loop(3, arrived)
            self.tip_w[...] = self.tip_r[...]
            for i in range(3):
                n = self.nf[4 + self.tip, self.face * 3 + i]
                group = lax.div(jnp.minimum(n, 11), 3)
                got = jnp.where(group == self.face, self.tip_s[0, pl.ds(i, 1)], self.tip_w[group, pl.ds(i, 1)])
                self.cells[self.tip, pl.ds(i, 1)] = jnp.where(n < 12, got, 0.0)

        not_, and_ = jnp.logical_not, jnp.logical_and
        for cell, flat, part, flat_side, upright, up_side in (
            (0, not_(self.left), 0, 3, not_(self.top), 0),
            (1, not_(self.right), 0, 1, not_(self.top), 0),
            (2, not_(self.right), 8, 1, not_(self.bottom), 2),
            (3, not_(self.left), 8, 3, not_(self.bottom), 2),
        ):
            @pl.when(flat)
            def _(cell=cell, part=part, flat_side=flat_side):
                self.cells[cell] = self.end_r[flat_side, pl.ds(part, 8)]

            @pl.when(and_(not_(flat), upright))
            def _(cell=cell, up_side=up_side):
                self.cells[cell] = self.end_r[up_side, pl.ds(0, 8)]

    def copy_end_ok(self, side):
        ok, dev = self.beside(side)
        return jnp.logical_and(ok, jnp.logical_or(lax.rem(side, 2) == 1, self.has_v))

    def wait_sends_a(self):
        loop(4, lambda k: self.sent(self.copy_beside(k)))
        loop(16, lambda k: self.sent(self.copy_class(k)))

    def wait_sends_b(self):
        loop(6, lambda k: self.sent(self.copy_across(k)))
        loop(3, lambda k: self.sent(self.copy_tip(k)))

    def wait_sends(self):
        loop(4, lambda k: self.sent(self.copy_end(k)))


EXCHANGE_SCRATCH = [
    pltpu.VMEM((2, 8, 3, 64, 128), BF16),
    pltpu.VMEM((2, 2, 4, 3, 64, 128), BF16),
    pltpu.VMEM((2, 2, 4, 3, 64, 128), BF16),
    pltpu.VMEM((2, 4, 8, 128), F32),
    pltpu.VMEM((2, 4, 8, 128), F32),
    pltpu.VMEM((2, 4, 16, 128), F32),
    pltpu.VMEM((2, 4, 16, 128), F32),
    pltpu.VMEM((8, 3, 64, 128), BF16), pltpu.VMEM((2, 4, 3, 64, 128), BF16), pltpu.VMEM((4, 8, 128), F32),
    pltpu.SemaphoreType.DMA((2, 4)), pltpu.SemaphoreType.DMA((2, 4)),
    pltpu.SemaphoreType.DMA((2, 2, 8)), pltpu.SemaphoreType.DMA((2, 8)),
    pltpu.SemaphoreType.DMA((2, 2, 4)), pltpu.SemaphoreType.DMA((2, 2, 4)),
    pltpu.SemaphoreType.DMA((2, 4)), pltpu.SemaphoreType.DMA((2, 4)),
    pltpu.SemaphoreType.DMA((2, 4)), pltpu.SemaphoreType.DMA((2, 4)),
]


PICK_AFTER = 2


def widen(w, out):
    out[...] = jnp.zeros(out.shape, BF16)
    for d in range(3):
        for p in range(2):
            for a in range(3):
                out[pl.ds((a + p) * 384 + d * 128, 128), pl.ds(p * 128, 128)] = w[a, d]


def build(f, img, xc, edges):
    col = lax.broadcasted_iota(jnp.int32, (8, 8, 128), 1)

    def rows(g):
        v = img[f, pl.ds(4 * g, 4)].reshape(8, 64, 128)
        wide = v.astype(F32)
        at = pl.ds(pl.multiple_of(8 * g, 8), 8)
        first = jnp.where(col == 0, edges[0, f, at][:, None, :], wide[:, 0:8])
        last = jnp.where(col == 7, edges[1, f, at][:, None, :], wide[:, 56:64])
        wide = jnp.concatenate([first, wide[:, 8:56], last], axis=1)
        parts = [pltpu.roll(wide, 1, 1).astype(BF16), wide.astype(BF16), pltpu.roll(wide, 63, 1).astype(BF16)]
        for i in range(8):
            k = 1 + i
            for d in range(3):
                xc[f, 4 * g + k // 2, k % 2, :, d * 128:(d + 1) * 128] = parts[d][i]

    loop(8, rows)


def inner(f, xc, w2, bias, img, after):
    def chunk(g):
        lhs = jnp.concatenate(
            [xc[f, pl.ds(PAIRS * g + t // 2, PAIRS), t % 2].reshape(PAIRS * 64, 384) for t in range(4)], axis=1)
        o = gelu(jnp.dot(lhs, w2[...], preferred_element_type=F32) + bias).astype(BF16)
        for p in range(2):
            img[f, pl.ds(PAIRS * g, PAIRS), p] = o[:, p * 128:(p + 1) * 128].reshape(PAIRS, 64, 128)
        after(32 // PAIRS * f + g)

    loop(32 // PAIRS, chunk)


SIDES = ((0, 3, 0, 128, 0), (1, 1, 256, 0, 62))


def ring_ready(f, xc, cols, g, rl, fix):
    for e, r, x0 in ((0, ((0, 1), (1, 0)), 384), (2, ((31, 1), (32, 0)), 0)):
        for k in range(2):
            rl[f, pl.ds(e * 64, 64), pl.ds(x0 + k * 384, 384)] = xc[f, r[k][0], r[k][1]]
    for side, e, rim, own, px in SIDES:
        for k in range(2):
            g[side, pl.ds(1, 64), pl.ds(k * 128, 128)] = cols[2 * side + k, f]
        for a in range(3):
            to = pl.ds(a * 384 + own, 256)
            rl[f, pl.ds(e * 64, 64), to] = g[side, pl.ds(a, 64)].astype(BF16)
            for tip, at in (((0, 1)[side], 0), ((3, 2)[side], 63)):
                fix[f, tip:tip + 1, to] = g[side, a + at:a + at + 1]


def ring(f, halo, rl, fix, w, bias, out):
    for e in range(4):
        mid = halo[e, f]
        wide = mid.astype(F32)
        parts = (pltpu.roll(wide, 1, 0).astype(BF16), mid, pltpu.roll(wide, 63, 0).astype(BF16))
        lane, step = ((0, 128), (256, 384), (768, 128), (0, 384))[e]
        for k in range(3):
            rl[f, pl.ds(e * 64, 64), pl.ds(lane + k * step, 128)] = parts[k]
        if e % 2 == 0:
            a = e * 384
            for side, _, rim, own, px in SIDES:
                tip = ((0, 1), (3, 2))[e // 2][side]
                for k in range(2):
                    fix[f, tip:tip + 1, pl.ds(a + own + k * 128, 128)] = wide[px + k:px + k + 1]
        else:
            for tip, a, at in (((1, 0)[e // 2], 384, 0), ((2, 3)[e // 2], 0, 62)):
                for k in range(2):
                    fix[f, tip:tip + 1, pl.ds(a + lane + k * 384, 128)] = wide[at + k:at + k + 1]
    out[f] = gelu(jnp.dot(rl[f], w, preferred_element_type=F32) + bias)


def corners(cells, fix, w, bias, out):
    for f in range(3):
        for tip, lane in ((0, 0), (1, 256), (2, 768 + 256), (3, 768)):
            fix[f, tip:tip + 1, pl.ds(lane, 128)] = cells[tip, f:f + 1]
    o = gelu(jnp.dot(fix[...].reshape(24, 1152).astype(BF16), w, preferred_element_type=F32) + bias)
    for f in range(3):
        for tip, at in ((0, 192), (1, 64), (2, 127), (3, 255)):
            out[f, at:at + 1] = o[8 * f + tip:8 * f + tip + 1]


def settle(f, o, out, edges):
    row = lax.broadcasted_iota(jnp.int32, (64, 128), 0)
    left, right = o[f, 192:256], o[f, 64:128]
    out[3, f] = left.astype(BF16)
    out[1, f] = right.astype(BF16)
    edges[0, f] = left
    edges[1, f] = right
    for e, k in ((0, 0), (2, 63)):
        line = jnp.where(row == 0, left[k:k + 1], jnp.where(row == 63, right[k:k + 1], o[f, e * 64:(e + 1) * 64]))
        out[e, f] = line.astype(BF16)


def main_kernel(x, nf_in, ori_in, w1, b1, w2, b2, skip, ring_out,
                img, nf, ori, xc, wv, bv, wide, lines, halo, cells, cols, edges, g, rl, fix, rims, load, store, *rest):
    bufs, seen, sems = rest[:7], rest[7:10], rest[10:]

    def exchange(layer):
        return Exchange(lines.at[layer], halo.at[layer], cells.at[layer], nf, ori,
                        *[b.at[layer] for b in bufs], [s.at[layer] for s in sems], seen)

    ends, middle = (pl.ds(0, 16), pl.ds(48, 16)), pl.ds(16, 32)
    moves = [pltpu.make_async_copy(src, dst, load.at[k]) for k, (src, dst) in enumerate((
        (x.at[:, :, :, ends[0]], img.at[:, :, :, ends[0]]), (x.at[:, :, :, ends[1]], img.at[:, :, :, ends[1]]),
        (x.at[:, 0, 0], lines.at[0, 0]), (x.at[:, 31, 1], lines.at[0, 2]),
        (x.at[:, :, :, middle], img.at[:, :, :, middle]),
        (w1, wv.at[0]), (b1, bv.at[0]), (nf_in, nf), (ori_in, ori), (w2, wv.at[1]), (b2, bv.at[1])))]
    for m in moves:
        m.start()
    exchange(0).greet()
    bufs[5][...] = jnp.zeros(bufs[5].shape, F32)
    bufs[3][...] = jnp.zeros(bufs[3].shape, F32)
    cells[...] = jnp.zeros(cells.shape, F32)
    fix[...] = jnp.zeros(fix.shape, F32)
    g[...] = jnp.zeros(g.shape, F32)

    def clear(f):
        xc[f, 0, 0] = jnp.zeros((64, 384), BF16)
        xc[f, 32, 1] = jnp.zeros((64, 384), BF16)

    loop(3, clear)
    for m in moves[:4]:
        m.wait()

    def first(f):
        near = img[f, :, :, 0:16].reshape(64, 16, 128).astype(F32)[:, 0]
        far = img[f, :, :, 48:64].reshape(64, 16, 128).astype(F32)[:, 15]
        edges[0, f] = near
        edges[1, f] = far
        lines[0, 3, f] = near.astype(BF16)
        lines[0, 1, f] = far.astype(BF16)

    loop(3, first)
    exchange(0).greeted()
    out = [pltpu.make_async_copy(img.at[f], skip.at[f], store.at[f]) for f in range(3)]

    def layer(k):
        ex = exchange(k)
        ex.start_a()

        @pl.when(k == 0)
        def _():
            for m in moves[4:]:
                m.wait()

        widen(wv.at[k], wide)
        bias = jnp.concatenate([bv[k], bv[k]], axis=1)

        def prepare(f):
            img[f, 0, 0] = lines[k, 0, f]
            img[f, 31, 1] = lines[k, 2, f]
            cols[0, f] = edges[0, f]
            cols[1, f] = img[f, :, :, 0:16].reshape(64, 16, 128).astype(F32)[:, 1]
            cols[2, f] = img[f, :, :, 48:64].reshape(64, 16, 128).astype(F32)[:, 14]
            cols[3, f] = edges[1, f]
            build(f, img, xc, edges)

        loop(3, prepare)

        def after(chunk):
            @pl.when(chunk == PICK_AFTER)
            def _():
                ex.stage_b()

        def face(f):
            inner(f, xc, wide, bias, img, after)

            @pl.when(k == 1)
            def _():
                pltpu.make_async_copy(img.at[f], skip.at[f], store.at[f]).start()

        loop(3, face)
        loop(3, lambda f: ring_ready(f, xc, cols, g, rl, fix))
        ex.wait_sends_a()
        ex.stage_c()
        ex.start_d()
        w = wv[k].reshape(1152, 128)
        loop(3, lambda f: ring(f, halo.at[k], rl, fix, w, bv[k], rims))
        ex.wait_sends_b()
        ex.finish()
        corners(cells.at[k], fix, w, bv[k], rims)
        loop(3, lambda f: settle(f, rims, lines.at[k + 1], edges))
        ex.wait_sends()

    loop(2, layer)
    ring_out[...] = lines[2]
    for o in out:
        o.wait()


def main(x, nf, ori, w1, b1, w2, b2):
    vm = pl.BlockSpec(memory_space=pltpu.VMEM)
    hbm = pl.BlockSpec(memory_space=pl.ANY)
    V = pltpu.VMEM
    return pl.pallas_call(
        main_kernel,
        in_specs=[hbm] * 7,
        out_specs=[hbm, vm],
        out_shape=[jax.ShapeDtypeStruct((3, 32, 2, 64, 128), BF16), jax.ShapeDtypeStruct((4, 3, 64, 128), BF16)],
        scratch_shapes=[
            V((3, 32, 2, 64, 128), BF16),
            pltpu.SMEM((8, 12), jnp.int32), pltpu.SMEM((8, 12), jnp.int32),
            V((3, 33, 2, 64, 384), BF16),
            V((2, 3, 3, 128, 128), BF16), V((2, 1, 128), F32),
            V((1536, 256), BF16),
            V((3, 4, 3, 64, 128), BF16), V((2, 4, 3, 64, 128), BF16),
            V((2, 4, 8, 128), F32),
            V((4, 3, 64, 128), F32), V((2, 3, 64, 128), F32),
            V((2, 72, 256), F32), V((3, 256, 1152), BF16),
            V((3, 8, 1152), F32), V((3, 256, 128), F32),
            pltpu.SemaphoreType.DMA((11,)), pltpu.SemaphoreType.DMA((3,)),
        ] + EXCHANGE_SCRATCH,
        compiler_params=pltpu.CompilerParams(collective_id=0, has_side_effects=True, vmem_limit_bytes=58 * 2**20),
    )(x.reshape(3, 32, 2, 64, 128), nf.T, ori.T, w1, b1.reshape(1, 128), w2, b2.reshape(1, 128))


def last_kernel(s, rim, wd_ref, bd_ref, out, coarse, wd, g32):
    f, g = pl.program_id(0), pl.program_id(1)
    P = s.shape[1]

    @pl.when(jnp.logical_and(f == 0, g == 0))
    def _():
        build_wd(wd_ref, wd)

    col = lax.broadcasted_iota(jnp.int32, (2 * P, 8, 128), 1)
    rows = pl.ds(pl.multiple_of(2 * P * g, 16), 2 * P)
    v = s[0].reshape(2 * P, 64, 128)
    wide = v.astype(F32)
    first = jnp.where(col == 0, rim[3, f, rows].astype(F32)[:, None, :], wide[:, 0:8])
    last = jnp.where(col == 7, rim[1, f, rows].astype(F32)[:, None, :], wide[:, 56:64])
    wide = jnp.concatenate([first, wide[:, 8:56], last], axis=1).reshape(P, 2, 64, 128)
    for a in range(2):
        g32[a] = wide[:, a].reshape(P * 64, 128)

    @pl.when(g == 0)
    def _():
        g32[0, 0:64] = rim[0, f].astype(F32)

    @pl.when(g == pl.num_programs(1) - 1)
    def _():
        g32[1, pl.ds((P - 1) * 64, 64)] = rim[2, f].astype(F32)

    for a in range(2):
        out[0, :, a] = g32[a].astype(BF16).reshape(P, 64, 128)
    parts = [g32[a, pl.ds(d, P * 32, stride=2), :] for d in range(2) for a in range(2)]
    q = jnp.concatenate(parts, axis=1).astype(BF16)
    cc = jnp.dot(q, wd[...], preferred_element_type=F32) + bd_ref[...]
    coarse[0] = cc.astype(BF16).reshape(P, 32, 256)


def last(s, rim, wd, bd, P=32):
    full = lambda *shape: pl.BlockSpec(shape, lambda f, g: (0,) * len(shape))
    block = pl.BlockSpec((1, P, 2, 64, 128), lambda f, g: (f, g, 0, 0, 0))
    skip, coarse = pl.pallas_call(
        last_kernel, grid=(3, 32 // P),
        in_specs=[block, full(4, 3, 64, 128), full(2, 2, 128, 256), full(1, 256)],
        out_specs=[block, pl.BlockSpec((1, P, 32, 256), lambda f, g: (f, g, 0, 0))],
        out_shape=[jax.ShapeDtypeStruct((3, 32, 2, 64, 128), BF16), jax.ShapeDtypeStruct((3, 32, 32, 256), BF16)],
        scratch_shapes=[pltpu.VMEM((512, 256), BF16), pltpu.VMEM((2, P * 64, 128), F32)],
        compiler_params=pltpu.CompilerParams(vmem_limit_bytes=58 * 2**20, dimension_semantics=("arbitrary", "arbitrary")),
    )(s, rim, wd, bd.reshape(1, 256))
    return skip.reshape(3, 64, 64, 128), coarse


def per_device(field, conv1_w, conv1_b, conv2_w, conv2_b, down_w, down_b, neighbour_face, orientation):
    s, rim = main(field, neighbour_face, orientation, conv1_w, conv1_b, conv2_w, conv2_b)
    return last(s, rim, down_w, down_b)


def solution(mesh):
    return jax.shard_map(
        per_device, mesh=mesh,
        in_specs=(P("face", "row", "col", None), P(), P(), P(), P(), P(), P(), P(), P()),
        out_specs=(P("face", "row", "col", None), P("face", "row", "col", None)),
        check_vma=False,
    )
```
